32 devices in a mesh: rows: 8 (over z, x), vocab: 4 (over y, core).
Axes of the slice: x: 2, y: 2, z: 4, core: 2. Of those that a mesh axis runs over, the one named last changes fastest.
Arguments:
- hidden_rows: bfloat16 [128, 8192], P('vocab', 'rows'), may hold values from -24 to 24
- row_states: int32 [128], P('vocab'), may hold values from 0 to 511
- head_weight: bfloat16 [8192, 152064], P(None, ('rows', 'vocab')), may hold values from -2 to 2
- grammar_table: int32 [512, 152064], P(None, ('rows', 'vocab')), may hold values from 0 to 1, as said below
Outputs:
- log_probs: float32 [128, 152064], P(None, ('rows', 'vocab'))
- normalizer: float32 [128], replicated
The draws below stay inside these ranges and needn't reach their ends.
Inputs may be any that keep to these rules, and one draw needn't show every extreme that they name: `grammar_table`: every state allows the tokens 0 to 31.
All inputs are finite; a program needn't handle non-finite values.
Results may differ from the reference program's by a relative error of at most 0.0003.
Values may be sent and summed in bfloat16 or wider, within the bound.
No kernel may reach another device: no remote copies, remote signals or barrier semaphores. Data moves between devices by JAX's collectives and lax.ppermute only.
A program may use at most 128 MiB of HBM per device.

```python
import math
import jax
import jax.numpy as jnp

D = 8192
VOCAB = 152064
STATES = 512
ROWS = 128


def draw_hidden_rows(key, part):
    key_scale = jax.random.fold_in(key, 11)
    key_values = jax.random.fold_in(key, 13)
    scales = jnp.exp(jax.random.uniform(key_scale, (ROWS, 1), minval=math.log(0.5), maxval=math.log(5.0)))
    entries = jnp.clip(jax.random.normal(key_values, (ROWS, D)), -4.0, 4.0) * scales
    return entries.astype(jnp.bfloat16)


def draw_head_weight(key, part):
    key_scale = jax.random.fold_in(key, 21)
    key_values = jax.random.fold_in(key, 22)
    col_scale = jnp.exp(jax.random.uniform(key_scale, (1, VOCAB), minval=math.log(0.4), maxval=math.log(4.0)))
    sample = jnp.clip(jax.random.normal(key_values, (D, VOCAB)), -4.0, 4.0)
    general = sample * col_scale / math.sqrt(D)
    block_rows = D // 32
    weight = 2.0 / math.sqrt(block_rows)
    special = jnp.where(jnp.arange(D)[:, None] // block_rows == jnp.arange(32)[None, :], weight, 0.0)
    return jnp.concatenate([special, general[:, 32:]], axis=1).astype(jnp.bfloat16)


def draw_grammar_table(key, part):
    key_rate = jax.random.fold_in(key, 31)
    key_tiles = jax.random.fold_in(key, 32)
    key_ticket = jax.random.fold_in(key, 33)
    tile_count = (VOCAB + 127) // 128
    thresh = jax.random.randint(key_rate, (STATES, 1), 16, 600)
    tile_flags = jax.random.randint(key_tiles, (STATES, tile_count), 0, 3) > 0
    tile_on = jnp.repeat(tile_flags, 128, axis=1)[:, :VOCAB]
    ticket = jax.random.randint(key_ticket, (STATES, VOCAB), 0, 1024)
    allowed = (ticket < thresh) & tile_on
    allowed = allowed | (jnp.arange(VOCAB)[None, :] < 32)
    return allowed.astype(jnp.int32)


def touch_ends(drawn, own_key, smallest, top_value):
    longest = drawn.shape.index(max(drawn.shape))
    spots = []
    for shift in (0, 1):
        where = [jax.random.randint(jax.random.fold_in(own_key, axis), (), 0, length) for axis, length in enumerate(drawn.shape)]
        where[longest] = (where[longest] + shift) % drawn.shape[longest]
        spots.append(tuple(where))
    return drawn.at[spots[0]].set(smallest).at[spots[1]].set(top_value)


def setup_inputs(seed: int = 0) -> dict:
    key_of = jax.random.split(jax.random.key(seed), 5)
    hidden_rows = draw_hidden_rows(jax.random.fold_in(key_of[4], 71), 0)
    row_states = touch_ends(jax.random.randint(key_of[1], (ROWS,), 0, STATES), jax.random.fold_in(key_of[1], 1), 0, STATES - 1).astype(jnp.int32)
    head_weight = draw_head_weight(jax.random.fold_in(key_of[4], 71), 0)
    grammar_table = draw_grammar_table(jax.random.fold_in(key_of[4], 71), 0)
    return {"hidden_rows": hidden_rows, "row_states": row_states, "head_weight": head_weight, "grammar_table": grammar_table}


lowest = -1.0e30


def reference(hidden_rows, row_states, head_weight, grammar_table):
    logits = jnp.dot(hidden_rows, head_weight, preferred_element_type=jnp.float32)
    allowed = jnp.take(grammar_table, row_states.astype(jnp.int32), axis=0) > 0
    masked = jnp.where(allowed, logits, lowest)
    row_peak = jnp.max(masked, axis=1)
    exp_total = jnp.sum(jnp.where(allowed, jnp.exp(logits - row_peak[:, None]), 0.0), axis=1)
    normalizer = row_peak + jnp.log(exp_total)
    log_probs = jnp.where(allowed, logits - normalizer[:, None], 0.0)
    return log_probs, normalizer
```

```python
import functools

import jax
import jax.numpy as jnp
from jax import lax
from jax.experimental import pallas as pl
from jax.experimental.pallas import tpu as pltpu
from jax.sharding import PartitionSpec as P

lowest = -1e30
reachable = -1e29
NT = (((1,), (1,)), ((), ()))


def ring_order(size):
    return list(range(0, size, 2)) + list(range(1, size, 2))[::-1]


def swap(x, axis, size, distance):
    return lax.ppermute(x, axis, [(i, i ^ distance) for i in range(size)])


def head_kernel(rows_count, vocab_count, columns, tile, where_ref, states_ref, *refs):
    own_refs = refs[:rows_count]
    other_refs = refs[rows_count : 2 * rows_count]
    weight_ref, table_ref, masked_ref, lse_ref, hidden, marks, peak, total = refs[2 * rows_count :]
    step = pl.program_id(0)
    half = vocab_count // 2
    block, depth = own_refs[0].shape[0] // half, own_refs[0].shape[1]
    all_rows = block * vocab_count
    state_count = table_ref.shape[1]

    @pl.when(step == 0)
    def _():
        core = where_ref[rows_count]
        for k in range(rows_count):
            at = pl.multiple_of(where_ref[k] * depth, depth)
            for j in range(half):
                mine = own_refs[k][j * block : (j + 1) * block, :]
                theirs = other_refs[k][j * block : (j + 1) * block, :]
                first = jnp.where(core == 0, mine, theirs)
                second = jnp.where(core == 0, theirs, mine)
                hidden[2 * j * block : (2 * j + 1) * block, pl.ds(at, depth)] = first
                hidden[(2 * j + 1) * block : (2 * j + 2) * block, pl.ds(at, depth)] = second
        state = lax.broadcasted_iota(jnp.int32, (state_count, all_rows), 0)
        marks[...] = (state == states_ref[...]).astype(jnp.float32).astype(jnp.bfloat16)
        peak[...] = jnp.full_like(peak, lowest)
        total[...] = jnp.zeros_like(total)

    logits = lax.dot_general(weight_ref[...], hidden[...], NT, preferred_element_type=jnp.float32)
    table = table_ref[...].astype(jnp.float32).astype(jnp.bfloat16)
    allowed = jnp.dot(table, marks[...], preferred_element_type=jnp.float32) > 0.5
    if columns % tile:
        token = step * tile + lax.broadcasted_iota(jnp.int32, (tile, 1), 0)
        allowed = jnp.logical_and(allowed, token < columns)
    masked = jnp.where(allowed, logits, lowest)
    masked_ref[...] = masked
    parts = masked.reshape(tile // 8, 8, all_rows)
    new_peak = jnp.maximum(peak[...], jnp.max(parts, axis=0))
    terms = jnp.where(parts > reachable, jnp.exp(parts - new_peak[None]), 0.0)
    total[...] = total[...] * jnp.exp(peak[...] - new_peak) + jnp.sum(terms, axis=0)
    peak[...] = new_peak

    @pl.when(step == pl.num_programs(0) - 1)
    def _():
        top = jnp.max(peak[...], axis=0, keepdims=True)
        whole = jnp.sum(total[...] * jnp.exp(peak[...] - top), axis=0, keepdims=True)
        lse_ref[...] = jnp.where(whole > 0.0, top + jnp.log(whole), lowest)


def combine(values):
    top = functools.reduce(jnp.maximum, values)
    terms = [jnp.exp(v - top) for v in values]
    while len(terms) > 1:
        terms = [terms[i] + terms[i + 1] for i in range(0, len(terms), 2)]
    return top + jnp.log(terms[0])


def local(rows_count, vocab_count, hidden_rows, row_states, head_weight, grammar_table):
    block, depth = hidden_rows.shape
    columns = head_weight.shape[1]
    state_count = grammar_table.shape[0]
    half = vocab_count // 2
    all_rows = block * vocab_count
    tile = 176
    row_at, vocab_at = lax.axis_index("rows"), lax.axis_index("vocab")
    core, chip = vocab_at % 2, vocab_at // 2

    def canonical(pieces, at):
        stacked = jnp.stack(pieces)
        if len(pieces) == 2:
            return jnp.where(at == 0, stacked, stacked[::-1])
        return jnp.take(stacked, jnp.arange(len(pieces)) ^ at, axis=0)

    own = canonical(
        [hidden_rows] + [swap(hidden_rows, "vocab", vocab_count, 2 * d) for d in range(1, half)], chip
    ).reshape(half * block, depth)
    states = [row_states] + [swap(row_states, "vocab", vocab_count, d) for d in range(1, vocab_count)]
    states = jnp.take(jnp.stack(states), jnp.arange(vocab_count) ^ vocab_at, axis=0).reshape(1, all_rows)

    order = ring_order(rows_count)
    ahead = [(order[i], order[(i + 1) % rows_count]) for i in range(rows_count)]
    back = [(b, a) for a, b in ahead]
    place = jnp.asarray(order, jnp.int32)
    spot = jnp.argmax(place == row_at).astype(jnp.int32)
    chunks, offsets = [own], [0]
    up = down = own
    for k in range(1, rows_count // 2 + 1):
        if k < rows_count // 2:
            up = lax.ppermute(up, "rows", ahead)
            down = lax.ppermute(down, "rows", back)
            chunks += [up, down]
            offsets += [-k, k]
        else:
            cut = half * block // 2
            last_up = lax.ppermute(up[:cut], "rows", ahead)
            last_down = lax.ppermute(down[cut:], "rows", back)
            chunks.append(jnp.concatenate([last_up, last_down]))
            offsets.append(k)
    others = [swap(c, "vocab", vocab_count, 1) for c in chunks]
    where = jnp.concatenate(
        [place[(spot + jnp.asarray(offsets, jnp.int32)) % rows_count], core[None].astype(jnp.int32)]
    )

    steps = pl.cdiv(columns, tile)
    whole = lambda shape: pl.BlockSpec(shape, lambda i, w: (0,) * len(shape))
    masked, lse = pl.pallas_call(
        functools.partial(head_kernel, rows_count, vocab_count, columns, tile),
        grid_spec=pltpu.PrefetchScalarGridSpec(
            num_scalar_prefetch=1,
            grid=(steps,),
            in_specs=[whole((1, all_rows))]
            + [whole((half * block, depth))] * (2 * rows_count)
            + [
                pl.BlockSpec((tile, depth * rows_count), lambda i, w: (i, 0)),
                pl.BlockSpec((tile, state_count), lambda i, w: (i, 0)),
            ],
            out_specs=[pl.BlockSpec((tile, all_rows), lambda i, w: (i, 0)), whole((1, all_rows))],
            scratch_shapes=[
                pltpu.VMEM((all_rows, depth * rows_count), jnp.bfloat16),
                pltpu.VMEM((state_count, all_rows), jnp.bfloat16),
                pltpu.VMEM((8, all_rows), jnp.float32),
                pltpu.VMEM((8, all_rows), jnp.float32),
            ],
        ),
        out_shape=[
            jax.ShapeDtypeStruct((columns, all_rows), jnp.float32),
            jax.ShapeDtypeStruct((1, all_rows), jnp.float32),
        ],
        compiler_params=pltpu.CompilerParams(
            dimension_semantics=("arbitrary",), vmem_limit_bytes=50 * 2**20
        ),
        cost_estimate=pl.CostEstimate(
            flops=2 * all_rows * depth * rows_count * columns,
            bytes_accessed=2 * depth * rows_count * columns + 4 * state_count * columns,
            transcendentals=all_rows * columns,
        ),
    )(where, states, *chunks, *others, head_weight.T, grammar_table.T)

    lse = combine([lse] + [swap(lse, "vocab", vocab_count, d) for d in range(1, vocab_count)])
    lse = combine([lse] + [swap(lse, "rows", rows_count, d) for d in range(1, rows_count)])
    log_probs = jnp.where(masked > reachable, masked - lse, 0.0)
    return log_probs.T, lse.reshape(all_rows)


def solution(mesh):
    placed = (
        P("vocab", "rows"),
        P("vocab"),
        P(None, ("rows", "vocab")),
        P(None, ("rows", "vocab")),
    )
    return jax.shard_map(
        functools.partial(local, mesh.shape["rows"], mesh.shape["vocab"]),
        mesh=mesh,
        in_specs=placed,
        out_specs=(P(None, ("rows", "vocab")), P()),
        check_vma=False,
    )
```

```python
import functools

import jax
import jax.numpy as jnp
from jax import lax
from jax.experimental import pallas as pl
from jax.experimental.pallas import tpu as pltpu
from jax.sharding import PartitionSpec as P

lowest = -1e30
reachable = -1e29
slots = 4


def ring_order(size):
    return list(range(0, size, 2)) + list(range(1, size, 2))[::-1]


def swap(x, axis, size, distance):
    return lax.ppermute(x, axis, [(i, i ^ distance) for i in range(size)])


def row_tile(columns):
    fits = [t for t in range(16, 529, 16) if columns % t == 0]
    return max(fits) if fits else columns


def ring_place(offset, count):
    here = lax.axis_index("rows")
    half = here // 2
    spot = jnp.where(here % 2 == 0, half, count - 1 - half)
    spot = lax.rem(spot + offset + count, count)
    return jnp.where(spot < count // 2, 2 * spot, 2 * (count - 1 - spot) + 1)


def stage_kernel(plan, *refs):
    rows_count, block, depth, columns, all_rows = plan["sizes"]
    refs = list(refs)
    take = lambda n: [refs.pop(0) for _ in range(n)]
    (weight,) = take(1)
    if plan["load_table"]:
        (table_in,) = take(1)
    else:
        take(1)
    if plan["first"]:
        states, table = take(plan["vocab_count"]), take(1)[0]
    elif plan["compute"]:
        take(1)
    chunks = [(slot, [(take(1)[0], *p) for p in pieces]) for slot, pieces in plan["compute"]]
    (held,) = take(1)
    acc = take(1)[0] if plan["compute"] else None
    lse = take(1)[0] if plan["last"] else None
    table_out = take(1)[0] if plan["load_table"] else None
    hidden, turned, marks, sems = take(4)

    tile = row_tile(columns)
    tiles = columns // tile
    copies = []
    for offset, slot in plan["load"]:
        at = pl.multiple_of(ring_place(offset, rows_count) * depth, depth)
        for t in range(tiles):
            span = pl.ds(t * tile, tile)
            copies.append((weight.at[span, pl.ds(at, depth)], held.at[slot, span, :]))
    if plan["load_table"]:
        for t in range(tiles):
            span = pl.ds(t * tile, tile)
            copies.append((table_in.at[span, :], table_out.at[span, :]))
    copies = [pltpu.make_async_copy(a, b, sems.at[n]) for n, (a, b) in enumerate(copies)]
    for copy in copies:
        copy.start()

    if plan["compute"]:
        vocab_at = lax.axis_index("vocab")
        for c, (_, pieces) in enumerate(chunks):
            for ref, first, other in pieces:
                for j in range(ref.shape[0] // block):
                    owner = vocab_at ^ (2 * (first + j) + other)
                    at = pl.multiple_of(owner * block, block)
                    hidden[pl.ds(at, block), :] = ref[j * block : (j + 1) * block, :]
            turned[c] = hidden[...].astype(jnp.float32).T.astype(jnp.bfloat16)
        if plan["first"]:
            state_count = table.shape[1]
            state = lax.broadcasted_iota(jnp.int32, (state_count, all_rows), 0)
            owner = lax.broadcasted_iota(jnp.int32, (1, all_rows), 1) // block
            wanted = jnp.zeros((1, all_rows), jnp.int32)
            for d, part in enumerate(states):
                wanted = jnp.where(owner == (vocab_at ^ d), jnp.tile(part[...], (1, all_rows // block)), wanted)
            marks[...] = (state == wanted).astype(jnp.float32).astype(jnp.bfloat16)

        def work(t, carry):
            span = pl.ds(pl.multiple_of(t * tile, tile), tile) if tiles > 1 else slice(None)
            if plan["first"]:
                rules = table[span, :].astype(jnp.float32).astype(jnp.bfloat16)
                allowed = jnp.dot(rules, marks[...], preferred_element_type=jnp.float32) > 0.5
                total = jnp.where(allowed, 0.0, lowest)
            else:
                total = acc[span, :]
            for c, (slot, _) in enumerate(chunks):
                total += jnp.dot(held[slot, span, :], turned[c], preferred_element_type=jnp.float32)
            acc[span, :] = total
            if plan["last"]:
                peak, exps = carry
                new_peak = jnp.maximum(peak, jnp.max(total, axis=0, keepdims=True))
                terms = jnp.where(total > reachable, jnp.exp(total - new_peak), 0.0)
                exps = exps * jnp.exp(peak - new_peak) + jnp.sum(terms, axis=0, keepdims=True)
                return new_peak, exps
            return carry

        start = ()
        if plan["last"]:
            start = (jnp.full((1, all_rows), lowest, jnp.float32), jnp.zeros((1, all_rows), jnp.float32))
        done = lax.fori_loop(0, tiles, work, start)
        if plan["last"]:
            peak, exps = done
            lse[...] = jnp.where(exps > 0.0, peak + jnp.log(exps), lowest)

    for copy in copies:
        copy.wait()


def stage(plan, weight, table_in, states, table, held, acc, chunks):
    rows_count, block, depth, columns, all_rows = plan["sizes"]
    vmem = pl.BlockSpec(memory_space=pltpu.VMEM)
    keep = lambda x: pltpu.with_memory_space_constraint(x, pltpu.VMEM)
    args, specs, out, alias = [weight], [pl.BlockSpec(memory_space=pl.ANY)], [], {}
    state_count = table_in.shape[1]
    if plan["load_table"]:
        args.append(pltpu.with_memory_space_constraint(table_in, pltpu.HBM))
        specs.append(pl.BlockSpec(memory_space=pltpu.HBM))
    else:
        alias[len(args)] = 0
        args.append(keep(held))
        specs.append(vmem)
    if plan["first"]:
        args += [*states, keep(table)]
        specs += [vmem] * (len(states) + 1)
    elif plan["compute"]:
        alias[len(args)] = 1
        args.append(keep(acc))
        specs.append(vmem)
    args += [p for pieces in chunks for p in pieces]
    specs += [vmem] * sum(len(pieces) for pieces in chunks)
    out.append(pltpu.VMEM((slots, columns, depth), jnp.bfloat16))
    if plan["compute"]:
        out.append(pltpu.VMEM((columns, all_rows), jnp.float32))
    if plan["last"]:
        out.append(jax.ShapeDtypeStruct((1, all_rows), jnp.float32))
    if plan["load_table"]:
        out.append(pltpu.VMEM((columns, state_count), jnp.int32))
    tiles = columns // row_tile(columns)
    moved = 2 * columns * depth * len(plan["load"]) + 4 * columns * state_count * plan["load_table"]
    return pl.pallas_call(
        functools.partial(stage_kernel, plan),
        in_specs=specs,
        out_shape=out,
        out_specs=[vmem] * len(out),
        input_output_aliases=alias,
        scratch_shapes=[
            pltpu.VMEM((all_rows, depth), jnp.bfloat16),
            pltpu.VMEM((max(1, len(plan["compute"])), depth, all_rows), jnp.bfloat16),
            pltpu.VMEM((state_count, all_rows), jnp.bfloat16),
            pltpu.SemaphoreType.DMA((max(1, tiles * (len(plan["load"]) + plan["load_table"])),)),
        ],
        compiler_params=pltpu.CompilerParams(vmem_limit_bytes=5 * 2**20),
        cost_estimate=pl.CostEstimate(
            flops=2 * all_rows * depth * columns * len(plan["compute"]),
            bytes_accessed=moved,
            transcendentals=all_rows * columns * plan["last"],
        ),
    )(*args)


def combine(a, b):
    top = jnp.maximum(a, b)
    return top + jnp.log(jnp.exp(a - top) + jnp.exp(b - top))


def local(rows_count, vocab_count, hidden_rows, row_states, head_weight, grammar_table):
    block, depth = hidden_rows.shape
    columns = head_weight.shape[1]
    half = vocab_count // 2
    all_rows = block * vocab_count
    weight, table_in = head_weight.T, grammar_table.T

    row_states = row_states.reshape(1, block)
    states = [row_states] + [swap(row_states, "vocab", vocab_count, d) for d in range(1, vocab_count)]
    own = jnp.concatenate(
        [hidden_rows] + [swap(hidden_rows, "vocab", vocab_count, 2 * d) for d in range(1, half)]
    )

    order = ring_order(rows_count)
    ahead = [(order[i], order[(i + 1) % rows_count]) for i in range(rows_count)]
    back = [(b, a) for a, b in ahead]
    hops = [[(0, [(own, 0)])]]
    up = down = own
    for k in range(1, rows_count // 2):
        up = lax.ppermute(up, "rows", ahead)
        down = lax.ppermute(down, "rows", back)
        hops.append([(-k, [(up, 0)]), (k, [(down, 0)])])
    hops.append([(rows_count // 2, [(lax.ppermute(up, "rows", ahead), 0)])])

    acc = table = held = None
    load, used = [], 0
    for j in range(len(hops) + 1):
        compute, chunks = [], []
        if j > 0:
            for (_, pieces), (_, slot) in zip(hops[j - 1], load):
                compute.append((slot, [(first, other) for _, first in pieces for other in (0, 1)]))
                chunks.append([a for p, _ in pieces for a in (p, swap(p, "vocab", vocab_count, 1))])
        load = []
        if j < len(hops):
            load = [(offset, (used + i) % slots) for i, (offset, _) in enumerate(hops[j])]
            used += len(load)
        plan = dict(
            vocab_count=vocab_count,
            sizes=(rows_count, block, depth, columns, all_rows),
            load=load,
            compute=compute,
            load_table=j == 0,
            first=j == 1,
            last=j == len(hops),
        )
        res = list(stage(plan, weight, table_in, states, table, held, acc, chunks))
        held = res.pop(0)
        if compute:
            acc = res.pop(0)
        if plan["last"]:
            lse = res.pop(0)
        if plan["load_table"]:
            table = res.pop(0)

    for axis, size in (("vocab", vocab_count), ("rows", rows_count)):
        distance = 1
        while distance < size:
            lse = combine(lse, swap(lse, axis, size, distance))
            distance *= 2
    log_probs = jnp.where(acc > reachable, acc - lse, 0.0)
    return log_probs.T, lse.reshape(all_rows)


def solution(mesh):
    placed = (
        P("vocab", "rows"),
        P("vocab"),
        P(None, ("rows", "vocab")),
        P(None, ("rows", "vocab")),
    )
    return jax.shard_map(
        functools.partial(local, mesh.shape["rows"], mesh.shape["vocab"]),
        mesh=mesh,
        in_specs=placed,
        out_specs=(P(None, ("rows", "vocab")), P()),
        check_vma=False,
    )
```

```python
import functools

import jax
import jax.numpy as jnp
from jax import lax
from jax.experimental import pallas as pl
from jax.experimental.pallas import tpu as pltpu
from jax.sharding import PartitionSpec as P

lowest = -1e30
reachable = -1e29
slots = 4


def ring_order(size):
    return list(range(0, size, 2)) + list(range(1, size, 2))[::-1]


def swap(x, axis, size, distance):
    return lax.ppermute(x, axis, [(i, i ^ distance) for i in range(size)])


def row_tile(columns):
    fits = [t for t in range(16, 529, 16) if columns % t == 0]
    return max(fits) if fits else columns


def ring_place(offset, count):
    here = lax.axis_index("rows")
    half = here // 2
    spot = jnp.where(here % 2 == 0, half, count - 1 - half)
    spot = lax.rem(spot + offset + count, count)
    return jnp.where(spot < count // 2, 2 * spot, 2 * (count - 1 - spot) + 1)


def stage_kernel(plan, *refs):
    rows_count, block, depth, columns, all_rows = plan["sizes"]
    refs = list(refs)
    take = lambda n: [refs.pop(0) for _ in range(n)]
    (weight,) = take(1)
    if plan["load_table"]:
        (table_in,) = take(1)
    else:
        take(1)
    if plan["first"]:
        states, table = take(plan["vocab_count"]), take(1)[0]
    elif plan["compute"]:
        take(1)
    chunks = [(slot, take(2)) for slot in plan["compute"]]
    (held,) = take(1)
    acc = take(1)[0] if plan["compute"] else None
    lse = take(1)[0] if plan["last"] else None
    table_out = take(1)[0] if plan["load_table"] else None
    hidden, turned, marks, sems = take(4)

    tile = row_tile(columns)
    tiles = columns // tile
    copies = []
    for offset, slot in plan["load"]:
        at = pl.multiple_of(ring_place(offset, rows_count) * depth, depth)
        for t in range(tiles):
            span = pl.ds(t * tile, tile)
            copies.append((weight.at[span, pl.ds(at, depth)], held.at[slot, span, :]))
    if plan["load_table"]:
        for t in range(tiles):
            span = pl.ds(t * tile, tile)
            copies.append((table_in.at[span, :], table_out.at[span, :]))
    copies = [pltpu.make_async_copy(a, b, sems.at[n]) for n, (a, b) in enumerate(copies)]
    for copy in copies:
        copy.start()

    if plan["compute"]:
        vocab_at = lax.axis_index("vocab")
        for c, (_, pieces) in enumerate(chunks):
            for other, ref in enumerate(pieces):
                for j in range(ref.shape[0] // block):
                    owner = vocab_at ^ (2 * j + other)
                    at = pl.multiple_of(owner * block, block)
                    hidden[pl.ds(at, block), :] = ref[j * block : (j + 1) * block, :]
            turned[c] = hidden[...].astype(jnp.float32).T.astype(jnp.bfloat16)
        if plan["first"]:
            state_count = table.shape[1]
            state = lax.broadcasted_iota(jnp.int32, (state_count, all_rows), 0)
            owner = lax.broadcasted_iota(jnp.int32, (1, all_rows), 1) // block
            wanted = jnp.zeros((1, all_rows), jnp.int32)
            for d, part in enumerate(states):
                wanted = jnp.where(owner == (vocab_at ^ d), jnp.tile(part[...], (1, all_rows // block)), wanted)
            marks[...] = (state == wanted).astype(jnp.float32).astype(jnp.bfloat16)

        def work(t, carry):
            span = pl.ds(pl.multiple_of(t * tile, tile), tile) if tiles > 1 else slice(None)
            if plan["first"]:
                rules = table[span, :].astype(jnp.float32).astype(jnp.bfloat16)
                allowed = jnp.dot(rules, marks[...], preferred_element_type=jnp.float32) > 0.5
                total = jnp.where(allowed, 0.0, lowest)
            else:
                total = acc[span, :]
            for c, (slot, _) in enumerate(chunks):
                total += jnp.dot(held[slot, span, :], turned[c], preferred_element_type=jnp.float32)
            acc[span, :] = total
            if plan["last"]:
                peak, exps = carry
                new_peak = jnp.maximum(peak, jnp.max(total, axis=0, keepdims=True))
                terms = jnp.where(total > reachable, jnp.exp(total - new_peak), 0.0)
                exps = exps * jnp.exp(peak - new_peak) + jnp.sum(terms, axis=0, keepdims=True)
                return new_peak, exps
            return carry

        start = ()
        if plan["last"]:
            start = (jnp.full((1, all_rows), lowest, jnp.float32), jnp.zeros((1, all_rows), jnp.float32))
        done = lax.fori_loop(0, tiles, work, start, unroll=True)
        if plan["last"]:
            peak, exps = done
            lse[...] = jnp.where(exps > 0.0, peak + jnp.log(exps), lowest)

    for copy in copies:
        copy.wait()


def stage(plan, weight, table_in, states, table, held, acc, chunks):
    rows_count, block, depth, columns, all_rows = plan["sizes"]
    vmem = pl.BlockSpec(memory_space=pltpu.VMEM)
    keep = lambda x: pltpu.with_memory_space_constraint(x, pltpu.VMEM)
    args, specs, out, alias = [weight], [pl.BlockSpec(memory_space=pl.ANY)], [], {}
    state_count = table_in.shape[1]
    if plan["load_table"]:
        args.append(pltpu.with_memory_space_constraint(table_in, pltpu.HBM))
        specs.append(pl.BlockSpec(memory_space=pltpu.HBM))
    else:
        alias[len(args)] = 0
        args.append(keep(held))
        specs.append(vmem)
    if plan["first"]:
        args += [*states, keep(table)]
        specs += [vmem] * (len(states) + 1)
    elif plan["compute"]:
        alias[len(args)] = 1
        args.append(keep(acc))
        specs.append(vmem)
    args += [p for pieces in chunks for p in pieces]
    specs += [vmem] * sum(len(pieces) for pieces in chunks)
    out.append(pltpu.VMEM((slots, columns, depth), jnp.bfloat16))
    if plan["compute"]:
        out.append(pltpu.VMEM((columns, all_rows), jnp.float32))
    if plan["last"]:
        out.append(jax.ShapeDtypeStruct((1, all_rows), jnp.float32))
    if plan["load_table"]:
        out.append(pltpu.VMEM((columns, state_count), jnp.int32))
    tiles = columns // row_tile(columns)
    moved = 2 * columns * depth * len(plan["load"]) + 4 * columns * state_count * plan["load_table"]
    return pl.pallas_call(
        functools.partial(stage_kernel, plan),
        in_specs=specs,
        out_shape=out,
        out_specs=[vmem] * len(out),
        input_output_aliases=alias,
        scratch_shapes=[
            pltpu.VMEM((all_rows, depth), jnp.bfloat16),
            pltpu.VMEM((max(1, len(plan["compute"])), depth, all_rows), jnp.bfloat16),
            pltpu.VMEM((state_count, all_rows), jnp.bfloat16),
            pltpu.SemaphoreType.DMA((max(1, tiles * (len(plan["load"]) + plan["load_table"])),)),
        ],
        compiler_params=pltpu.CompilerParams(vmem_limit_bytes=5 * 2**20),
        cost_estimate=pl.CostEstimate(
            flops=2 * all_rows * depth * columns * len(plan["compute"]),
            bytes_accessed=moved,
            transcendentals=all_rows * columns * plan["last"],
        ),
    )(*args)


def join_kernel(*refs):
    size = refs[0].shape[0]
    for i, ref in enumerate(refs[:-1]):
        refs[-1][i * size : (i + 1) * size, :] = ref[...]


def join(parts):
    rows, width = parts[0].shape
    return pl.pallas_call(
        join_kernel,
        in_specs=[pl.BlockSpec(memory_space=pltpu.VMEM)] * len(parts),
        out_specs=pl.BlockSpec(memory_space=pltpu.VMEM),
        out_shape=jax.ShapeDtypeStruct((rows * len(parts), width), parts[0].dtype),
        compiler_params=pltpu.CompilerParams(vmem_limit_bytes=2 * 2**20),
    )(*parts)


def local(rows_count, vocab_count, hidden_rows, row_states, head_weight, grammar_table):
    block, depth = hidden_rows.shape
    columns = head_weight.shape[1]
    half = vocab_count // 2
    all_rows = block * vocab_count
    weight, table_in = head_weight.T, grammar_table.T

    row_states = row_states.reshape(1, block)
    states = [row_states] + [swap(row_states, "vocab", vocab_count, d) for d in range(1, vocab_count)]
    own = [hidden_rows] + [swap(hidden_rows, "vocab", vocab_count, 2 * d) for d in range(1, half)]
    plan = dict(
        vocab_count=vocab_count,
        sizes=(rows_count, block, depth, columns, all_rows),
        load=[(0, 0)],
        compute=[],
        load_table=True,
        first=False,
        last=False,
    )
    held, table = stage(plan, weight, table_in, states, None, None, None, [])
    own, states, held, table = lax.optimization_barrier((own, states, held, table))
    own = join(own)

    order = ring_order(rows_count)
    ahead = [(order[i], order[(i + 1) % rows_count]) for i in range(rows_count)]
    back = [(b, a) for a, b in ahead]
    last_hop = rows_count // 2
    acc, load, used = None, plan["load"], 1
    arrived = [(0, own)]
    up = down = own
    for j in range(1, last_hop + 2):
        coming = []
        if j < last_hop:
            coming = [(-j, lax.ppermute(up, "rows", ahead)), (j, lax.ppermute(down, "rows", back))]
        elif j == last_hop:
            coming = [(j, lax.ppermute(up, "rows", ahead))]
        compute = [slot for _, slot in load]
        chunks = [[piece, swap(piece, "vocab", vocab_count, 1)] for _, piece in arrived]
        load = [(offset, (used + i) % slots) for i, (offset, _) in enumerate(coming)]
        used += len(load)
        plan = dict(
            vocab_count=vocab_count,
            sizes=(rows_count, block, depth, columns, all_rows),
            load=load,
            compute=compute,
            load_table=False,
            first=j == 1,
            last=j > last_hop,
        )
        res = list(stage(plan, weight, table_in, states, table, held, acc, chunks))
        held, acc = res[:2]
        if plan["last"]:
            lse = res[2]
        else:
            pieces, held, acc = lax.optimization_barrier(([p for _, p in coming], held, acc))
            arrived = [(offset, p) for (offset, _), p in zip(coming, pieces)]
            up, down = pieces[0], pieces[-1]

    count = rows_count * vocab_count
    sent = jnp.broadcast_to(lse[None], (count, 1, all_rows))
    parts = lax.all_to_all(sent, ("rows", "vocab"), 0, 0, tiled=True)
    top = jnp.max(parts, axis=0)
    lse = top + jnp.log(jnp.sum(jnp.exp(parts - top), axis=0))
    log_probs = jnp.where(acc > reachable, acc - lse, 0.0)
    return log_probs.T, lse.reshape(all_rows)


def solution(mesh):
    placed = (
        P("vocab", "rows"),
        P("vocab"),
        P(None, ("rows", "vocab")),
        P(None, ("rows", "vocab")),
    )
    return jax.shard_map(
        functools.partial(local, mesh.shape["rows"], mesh.shape["vocab"]),
        mesh=mesh,
        in_specs=placed,
        out_specs=(P(None, ("rows", "vocab")), P()),
        check_vma=False,
    )
```

```python
import functools

import jax
import jax.numpy as jnp
from jax import lax
from jax.experimental import pallas as pl
from jax.experimental.pallas import tpu as pltpu
from jax.sharding import PartitionSpec as P

lowest = -1e30
reachable = -1e29
slots = 4


def ring_order(size):
    return list(range(0, size, 2)) + list(range(1, size, 2))[::-1]


def swap(x, axis, size, distance):
    return lax.ppermute(x, axis, [(i, i ^ distance) for i in range(size)])


def row_tile(columns):
    fits = [t for t in range(16, 529, 16) if columns % t == 0]
    return max(fits) if fits else columns


def ring_place(offset, count):
    here = lax.axis_index("rows")
    half = here // 2
    spot = jnp.where(here % 2 == 0, half, count - 1 - half)
    spot = lax.rem(spot + offset + count, count)
    return jnp.where(spot < count // 2, 2 * spot, 2 * (count - 1 - spot) + 1)


def load_plan(hops, tiles):
    units = [(j, c, t) for j, hop in enumerate(hops) for t in range(tiles) for c in hop]
    wanted = [0.75 * tiles * len(hop) for hop in hops]
    wanted[0] += 1.2 * tiles
    wanted[-1] += 0.2 * tiles
    ready = max(0.0, len(units) - sum(wanted))
    stage_of = {c: j + 1 for j, hop in enumerate(hops) for c in hop}
    plan, used, upto = [], 0, ready
    needed = 0
    for j in range(len(hops) + 1):
        if j > 0:
            upto += wanted[j - 1]
            needed += tiles * len(hops[j - 1])
        end = min(len(units), max(int(round(upto)), needed))
        while any(c >= slots and stage_of[c - slots] >= j for _, c, _ in units[used:end]):
            end -= 1
        assert end >= needed
        plan.append(units[used:end])
        used = max(used, end)
    return plan


def stage_kernel(plan, *refs):
    rows_count, block, depth, columns, all_rows = plan["sizes"]
    refs = list(refs)
    take = lambda n: [refs.pop(0) for _ in range(n)]
    (weight,) = take(1)
    if plan["first"]:
        states, rules_in = take(plan["vocab_count"]), take(1)[0]
    if not plan["compute"]:
        (table,) = take(1)
    else:
        take(1 if plan["first"] else 2)
    chunks = [(slot, take(2)) for slot in plan["compute"]]
    (held,) = take(1)
    acc = take(1)[0] if plan["compute"] else None
    lse = take(1)[0] if plan["last"] else None
    if plan["compute"]:
        hidden, turned, marks, sems = take(4)
    else:
        rules_out, raw, raw_sems, sems = take(4)

    tile = row_tile(columns)
    tiles = columns // tile
    if not plan["compute"]:
        raw_copies = []
        for t in range(tiles):
            span = pl.ds(t * tile, tile)
            raw_copies.append(pltpu.make_async_copy(table.at[span, :], raw.at[t % 3], raw_sems.at[t]))
        for copy in raw_copies[:3]:
            copy.start()
    copies = {}
    places = {offset: ring_place(offset, rows_count) for offset, _, _ in plan["load"]}
    for n, (offset, slot, t) in enumerate(plan["load"]):
        at = pl.multiple_of(places[offset] * depth, depth)
        span = pl.ds(t * tile, tile)
        copy = pltpu.make_async_copy(weight.at[span, pl.ds(at, depth)], held.at[slot, span, :], sems.at[n])
        copy.start()
        copies[slot, t] = copy

    if plan["compute"]:
        vocab_at = lax.axis_index("vocab")
        for c, (_, pieces) in enumerate(chunks):
            for other, ref in enumerate(pieces):
                for j in range(ref.shape[0] // block):
                    owner = vocab_at ^ (2 * j + other)
                    at = pl.multiple_of(owner * block, block)
                    hidden[pl.ds(at, block), :] = ref[j * block : (j + 1) * block, :]
            turned[c] = hidden[...].astype(jnp.float32).T.astype(jnp.bfloat16)
        if plan["first"]:
            state_count = rules_in.shape[1]
            state = lax.broadcasted_iota(jnp.int32, (state_count, all_rows), 0)
            owner = lax.broadcasted_iota(jnp.int32, (1, all_rows), 1) // block
            wanted = jnp.zeros((1, all_rows), jnp.int32)
            for d, part in enumerate(states):
                wanted = jnp.where(owner == (vocab_at ^ d), jnp.tile(part[...], (1, all_rows // block)), wanted)
            marks[...] = (state == wanted).astype(jnp.float32).astype(jnp.bfloat16)

        peak = jnp.full((1, all_rows), lowest, jnp.float32)
        exps = jnp.zeros((1, all_rows), jnp.float32)
        for t in range(tiles):
            span = pl.ds(t * tile, tile)
            if plan["first"]:
                allowed = jnp.dot(rules_in[span, :], marks[...], preferred_element_type=jnp.float32) > 0.5
                total = jnp.where(allowed, 0.0, lowest)
            else:
                total = acc[span, :]
            for c, (slot, _) in enumerate(chunks):
                if (slot, t) in copies:
                    copies.pop((slot, t)).wait()
                total += jnp.dot(held[slot, span, :], turned[c], preferred_element_type=jnp.float32)
            acc[span, :] = total
            if plan["last"]:
                new_peak = jnp.maximum(peak, jnp.max(total, axis=0, keepdims=True))
                terms = jnp.where(total > reachable, jnp.exp(total - new_peak), 0.0)
                exps = exps * jnp.exp(peak - new_peak) + jnp.sum(terms, axis=0, keepdims=True)
                peak = new_peak
        if plan["last"]:
            lse[...] = jnp.where(exps > 0.0, peak + jnp.log(exps), lowest)

    else:
        for t in range(tiles):
            raw_copies[t].wait()
            rules_out[pl.ds(t * tile, tile), :] = raw[t % 3].astype(jnp.float32).astype(jnp.bfloat16)
            if t + 3 < tiles:
                raw_copies[t + 3].start()

    for copy in copies.values():
        copy.wait()


def stage(plan, weight, states, table, rules, held, acc, chunks):
    rows_count, block, depth, columns, all_rows = plan["sizes"]
    vmem = pl.BlockSpec(memory_space=pltpu.VMEM)
    keep = lambda x: pltpu.with_memory_space_constraint(x, pltpu.VMEM)
    args, specs, out, alias = [weight], [pl.BlockSpec(memory_space=pl.ANY)], [], {}
    tile, state_count = row_tile(columns), table.shape[1]
    if plan["first"]:
        args += [*states, keep(rules)]
    if not plan["compute"]:
        args.append(pltpu.with_memory_space_constraint(table, pltpu.HBM))
        specs.append(pl.BlockSpec(memory_space=pltpu.HBM))
    else:
        alias[len(args)] = 0
        args.append(keep(held))
        if not plan["first"]:
            alias[len(args)] = 1
            args.append(keep(acc))
    args += [p for pieces in chunks for p in pieces]
    specs += [vmem] * (len(args) - len(specs))
    out.append(pltpu.VMEM((slots, columns, depth), jnp.bfloat16))
    if plan["compute"]:
        out.append(pltpu.VMEM((columns, all_rows), jnp.float32))
    if plan["last"]:
        out.append(jax.ShapeDtypeStruct((1, all_rows), jnp.float32))
    sems = pltpu.SemaphoreType.DMA((max(1, len(plan["load"])),))
    if plan["compute"]:
        scratch = [
            pltpu.VMEM((all_rows, depth), jnp.bfloat16),
            pltpu.VMEM((len(plan["compute"]), depth, all_rows), jnp.bfloat16),
            pltpu.VMEM((state_count, all_rows), jnp.bfloat16),
            sems,
        ]
    else:
        out.append(pltpu.VMEM((columns, state_count), jnp.bfloat16))
        scratch = [
            pltpu.VMEM((3, tile, state_count), jnp.int32),
            pltpu.SemaphoreType.DMA((columns // tile,)),
            sems,
        ]
    moved = 2 * tile * depth * len(plan["load"])
    return pl.pallas_call(
        functools.partial(stage_kernel, plan),
        in_specs=specs,
        out_shape=out,
        out_specs=[vmem] * len(out),
        input_output_aliases=alias,
        scratch_shapes=scratch,
        compiler_params=pltpu.CompilerParams(vmem_limit_bytes=6 * 2**20),
        cost_estimate=pl.CostEstimate(
            flops=2 * all_rows * depth * columns * len(plan["compute"]),
            bytes_accessed=moved,
            transcendentals=all_rows * columns * plan["last"],
        ),
    )(*args)


def join_kernel(*refs):
    size = refs[0].shape[0]
    for i, ref in enumerate(refs[:-1]):
        refs[-1][i * size : (i + 1) * size, :] = ref[...]


def join(parts):
    rows, width = parts[0].shape
    return pl.pallas_call(
        join_kernel,
        in_specs=[pl.BlockSpec(memory_space=pltpu.VMEM)] * len(parts),
        out_specs=pl.BlockSpec(memory_space=pltpu.VMEM),
        out_shape=jax.ShapeDtypeStruct((rows * len(parts), width), parts[0].dtype),
        compiler_params=pltpu.CompilerParams(vmem_limit_bytes=2 * 2**20),
    )(*parts)


def local(rows_count, vocab_count, hidden_rows, row_states, head_weight, grammar_table):
    block, depth = hidden_rows.shape
    columns = head_weight.shape[1]
    half = vocab_count // 2
    all_rows = block * vocab_count
    weight, table = head_weight.T, grammar_table.T

    row_states = row_states.reshape(1, block)
    states = [row_states] + [swap(row_states, "vocab", vocab_count, d) for d in range(1, vocab_count)]
    own = [hidden_rows] + [swap(hidden_rows, "vocab", vocab_count, 2 * d) for d in range(1, half)]
    last_hop = rows_count // 2
    offsets = [0] + [s * j for j in range(1, last_hop) for s in (-1, 1)] + [last_hop]
    hops = [[0]] + [[2 * j - 1, 2 * j] for j in range(1, last_hop)] + [[rows_count - 1]]
    loads = load_plan(hops, columns // row_tile(columns))

    def planned(j):
        return dict(
            vocab_count=vocab_count,
            sizes=(rows_count, block, depth, columns, all_rows),
            load=[(offsets[c], c % slots, t) for _, c, t in loads[j]],
            compute=[c % slots for c in hops[j - 1]] if j else [],
            first=j == 1,
            last=j > last_hop,
        )

    held, rules = stage(planned(0), weight, None, table, None, None, None, [])
    own, states, held, rules = lax.optimization_barrier((own, states, held, rules))
    own = join(own)

    order = ring_order(rows_count)
    ahead = [(order[i], order[(i + 1) % rows_count]) for i in range(rows_count)]
    back = [(b, a) for a, b in ahead]
    acc = None
    arrived = [own]
    up = down = own
    for j in range(1, last_hop + 2):
        coming = []
        if j < last_hop:
            coming = [lax.ppermute(up, "rows", ahead), lax.ppermute(down, "rows", back)]
        elif j == last_hop:
            coming = [lax.ppermute(up, "rows", ahead)]
        chunks = [[piece, swap(piece, "vocab", vocab_count, 1)] for piece in arrived]
        held, acc, *rest = stage(planned(j), weight, states, table, rules, held, acc, chunks)
        if coming:
            arrived, held, acc = lax.optimization_barrier((coming, held, acc))
            up, down = arrived[0], arrived[-1]

    (lse,) = rest
    count = rows_count * vocab_count
    sent = jnp.broadcast_to(lse[None], (count, 1, all_rows))
    parts = lax.all_to_all(sent, ("rows", "vocab"), 0, 0, tiled=True)
    top = jnp.max(parts, axis=0)
    lse = top + jnp.log(jnp.sum(jnp.exp(parts - top), axis=0))
    log_probs = jnp.where(acc > reachable, acc - lse, 0.0)
    return log_probs.T, lse.reshape(all_rows)


def solution(mesh):
    placed = (
        P("vocab", "rows"),
        P("vocab"),
        P(None, ("rows", "vocab")),
        P(None, ("rows", "vocab")),
    )
    return jax.shard_map(
        functools.partial(local, mesh.shape["rows"], mesh.shape["vocab"]),
        mesh=mesh,
        in_specs=placed,
        out_specs=(P(None, ("rows", "vocab")), P()),
        check_vma=False,
    )
```

```python
import functools

import jax
import jax.numpy as jnp
from jax import lax
from jax.experimental import pallas as pl
from jax.experimental.pallas import tpu as pltpu
from jax.sharding import PartitionSpec as P

lowest = -1e30
reachable = -1e29
slots = 4
NT = (((1,), (1,)), ((), ()))


def ring_order(size):
    return list(range(0, size, 2)) + list(range(1, size, 2))[::-1]


def swap(x, axis, size, distance):
    return lax.ppermute(x, axis, [(i, i ^ distance) for i in range(size)])


def row_spans(columns):
    if columns % 16:
        return [(0, columns)]
    return [(t, min(512, columns - t)) for t in range(0, columns, 512)]


def up_to(size, step):
    return -(-size // step) * step


def ring_place(offset, count):
    here = lax.axis_index("rows")
    half = here // 2
    spot = jnp.where(here % 2 == 0, half, count - 1 - half)
    spot = lax.rem(spot + offset + count, count)
    return jnp.where(spot < count // 2, 2 * spot, 2 * (count - 1 - spot) + 1)


def stage_kernel(plan, *refs):
    rows_count, block, depth, columns, all_rows = plan["sizes"]
    half = plan["vocab_count"] // 2
    refs = list(refs)
    take = lambda n: [refs.pop(0) for _ in range(n)]
    (weight,) = take(1)
    if plan["first"]:
        (rules_in,) = take(1)
    if not plan["compute"]:
        (table,) = take(1)
    else:
        take(1 if plan["first"] else 2)
    chunks = [(slot, take(2)) for slot in plan["compute"]]
    (held,) = take(1)
    acc = take(1)[0] if plan["compute"] else None
    turned, lse = take(2) if plan["last"] else (None, None)
    if plan["compute"]:
        hidden, marks, sems = take(3)
    else:
        rules_out, raw, raw_sems, sems = take(4)

    spans = row_spans(columns)
    copies = []
    if not plan["compute"]:
        raw_copies = []
        for t, (begin, size) in enumerate(spans):
            part = raw.at[t % 3, pl.ds(0, size), :]
            raw_copies.append(pltpu.make_async_copy(table.at[pl.ds(begin, size), :], part, raw_sems.at[t]))
        for copy in raw_copies[:3]:
            copy.start()
    for offset, slot in plan["load"]:
        at = pl.multiple_of(ring_place(offset, rows_count) * depth, depth)
        for begin, size in spans:
            span = pl.ds(begin, size)
            source = weight.at[span, pl.ds(at, depth)]
            copies.append(pltpu.make_async_copy(source, held.at[slot, span, :], sems.at[len(copies)]))
            copies[-1].start()

    if plan["compute"]:
        vocab_at = lax.axis_index("vocab")
        for c, (_, pieces) in enumerate(chunks):
            for other, ref in enumerate(pieces):
                for j in range(half):
                    at = pl.multiple_of((vocab_at ^ (2 * j + other)) * block, block)
                    hidden[c, pl.ds(at, block), :] = ref[j * block : (j + 1) * block, :]
        if plan["first"]:
            state_count = rules_in.shape[1]
            owner = lax.broadcasted_iota(jnp.int32, (1, all_rows), 1) // block
            wanted = jnp.zeros((1, all_rows), jnp.float32)
            for other, ref in enumerate(chunks[0][1]):
                digits = ref[half * block :, : up_to(half * block, 128)].astype(jnp.float32)
                states = digits[0:1] * 256.0 + digits[1:2]
                for j in range(half):
                    part = jnp.tile(states[:, j * block : (j + 1) * block], (1, all_rows // block))
                    wanted = jnp.where(owner == (vocab_at ^ (2 * j + other)), part, wanted)
            state = lax.broadcasted_iota(jnp.int32, (state_count, all_rows), 0).astype(jnp.float32)
            marks[...] = (state == wanted).astype(jnp.float32).T.astype(jnp.bfloat16)

        peak = jnp.full((all_rows, 1), lowest, jnp.float32)
        exps = jnp.zeros((all_rows, 1), jnp.float32)
        for begin, size in spans:
            span = pl.ds(begin, size)
            if plan["first"]:
                hits = lax.dot_general(marks[...], rules_in[span, :], NT, preferred_element_type=jnp.float32)
                total = jnp.where(hits > 0.5, 0.0, lowest)
            else:
                total = acc[:, span]
            for c, (slot, _) in enumerate(chunks):
                total += lax.dot_general(hidden[c], held[slot, span, :], NT, preferred_element_type=jnp.float32)
            if not plan["last"]:
                acc[:, span] = total
            else:
                turned[span, :] = total.T
                new_peak = jnp.maximum(peak, jnp.max(total, axis=1, keepdims=True))
                terms = jnp.where(total > reachable, jnp.exp(total - new_peak), 0.0)
                exps = exps * jnp.exp(peak - new_peak) + jnp.sum(terms, axis=1, keepdims=True)
                peak = new_peak
        if plan["last"]:
            found = jnp.where(exps > 0.0, peak + jnp.log(exps), lowest)
            lse[...] = jnp.broadcast_to(found, (all_rows, 128)).T[0:1, :]
    else:
        for t, (begin, size) in enumerate(spans):
            raw_copies[t].wait()
            rules_out[pl.ds(begin, size), :] = raw[t % 3, :size].astype(jnp.float32).astype(jnp.bfloat16)
            if t + 3 < len(spans):
                raw_copies[t + 3].start()

    for copy in copies:
        copy.wait()


def stage(plan, weight, table, rules, held, acc, chunks):
    rows_count, block, depth, columns, all_rows = plan["sizes"]
    vmem = pl.BlockSpec(memory_space=pltpu.VMEM)
    keep = lambda x: pltpu.with_memory_space_constraint(x, pltpu.VMEM)
    args, specs, out, alias = [weight], [pl.BlockSpec(memory_space=pl.ANY)], [], {}
    spans, state_count = row_spans(columns), table.shape[1]
    if plan["first"]:
        args.append(keep(rules))
        specs.append(vmem)
    if not plan["compute"]:
        args.append(pltpu.with_memory_space_constraint(table, pltpu.HBM))
        specs.append(pl.BlockSpec(memory_space=pltpu.HBM))
    else:
        alias[len(args)] = 0
        args.append(keep(held))
        if not plan["first"]:
            alias[len(args)] = 1
            args.append(keep(acc))
    args += [p for pieces in chunks for p in pieces]
    specs += [vmem] * (len(args) - len(specs))
    out.append(pltpu.VMEM((slots, columns, depth), jnp.bfloat16))
    if plan["compute"]:
        out.append(pltpu.VMEM((all_rows, up_to(columns, 128)), jnp.float32))
    if plan["last"]:
        out.append(pltpu.VMEM((columns, all_rows), jnp.float32))
        out.append(jax.ShapeDtypeStruct((1, all_rows), jnp.float32))
    sems = pltpu.SemaphoreType.DMA((max(1, len(plan["load"]) * len(spans)),))
    if plan["compute"]:
        scratch = [
            pltpu.VMEM((len(plan["compute"]), all_rows, depth), jnp.bfloat16),
            pltpu.VMEM((all_rows, state_count), jnp.bfloat16),
            sems,
        ]
    else:
        out.append(pltpu.VMEM((columns, state_count), jnp.bfloat16))
        scratch = [
            pltpu.VMEM((3, spans[0][1], state_count), jnp.int32),
            pltpu.SemaphoreType.DMA((len(spans),)),
            sems,
        ]
    return pl.pallas_call(
        functools.partial(stage_kernel, plan),
        in_specs=specs,
        out_shape=out,
        out_specs=[vmem] * len(out),
        input_output_aliases=alias,
        scratch_shapes=scratch,
        compiler_params=pltpu.CompilerParams(vmem_limit_bytes=6 * 2**20),
        cost_estimate=pl.CostEstimate(
            flops=2 * all_rows * depth * columns * len(plan["compute"]),
            bytes_accessed=2 * columns * depth * len(plan["load"]),
            transcendentals=all_rows * columns * plan["last"],
        ),
    )(*args)


def join_kernel(half, *refs):
    pieces, states, (plain, marked) = refs[:half], refs[half : 2 * half], refs[2 * half :]
    block = pieces[0].shape[0]
    for j, ref in enumerate(pieces):
        plain[j * block : (j + 1) * block, :] = ref[...]
        marked[j * block : (j + 1) * block, :] = ref[...]
    width = up_to(half * block, 128)
    owner = lax.broadcasted_iota(jnp.int32, (1, width), 1) // block
    joined = jnp.zeros((1, width), jnp.int32)
    for j, ref in enumerate(states):
        joined = jnp.where(owner == j, jnp.tile(ref[...], (1, width // block)), joined)
    digit = lax.broadcasted_iota(jnp.int32, (16, width), 0)
    digits = jnp.where(digit == 0, joined // 256, jnp.where(digit == 1, joined % 256, 0))
    marked[half * block :, :width] = digits.astype(jnp.float32).astype(jnp.bfloat16)


def join(pieces, states):
    block, depth = pieces[0].shape
    rows = block * len(pieces)
    vmem = pl.BlockSpec(memory_space=pltpu.VMEM)
    return pl.pallas_call(
        functools.partial(join_kernel, len(pieces)),
        in_specs=[vmem] * (2 * len(pieces)),
        out_specs=[vmem] * 2,
        out_shape=[
            jax.ShapeDtypeStruct((rows, depth), jnp.bfloat16),
            jax.ShapeDtypeStruct((rows + 16, depth), jnp.bfloat16),
        ],
        compiler_params=pltpu.CompilerParams(vmem_limit_bytes=4 * 2**20),
    )(*pieces, *states)


def local(rows_count, vocab_count, hidden_rows, row_states, head_weight, grammar_table):
    block, depth = hidden_rows.shape
    columns = head_weight.shape[1]
    half = vocab_count // 2
    all_rows = block * vocab_count
    weight, table = head_weight.T, grammar_table.T

    row_states = row_states.reshape(1, block)
    shared = lambda x: [x] + [swap(x, "vocab", vocab_count, 2 * d) for d in range(1, half)]
    pieces, states = shared(hidden_rows), shared(row_states)
    last_hop = rows_count // 2
    offsets = [0] + [s * j for j in range(1, last_hop) for s in (-1, 1)] + [last_hop]
    hops = [[0]] + [[2 * j - 1, 2 * j] for j in range(1, last_hop)] + [[rows_count - 1]]

    def planned(j):
        return dict(
            vocab_count=vocab_count,
            sizes=(rows_count, block, depth, columns, all_rows),
            load=[(offsets[c], c % slots) for c in hops[j]] if j <= last_hop else [],
            compute=[c % slots for c in hops[j - 1]] if j else [],
            first=j == 1,
            last=j > last_hop,
        )

    held, rules = stage(planned(0), weight, table, None, None, None, [])
    pieces, states, held, rules = lax.optimization_barrier((pieces, states, held, rules))
    own, marked = join(pieces, states)

    order = ring_order(rows_count)
    ahead = [(order[i], order[(i + 1) % rows_count]) for i in range(rows_count)]
    back = [(b, a) for a, b in ahead]
    acc = None
    arrived = [marked]
    up = down = own
    for j in range(1, last_hop + 2):
        coming = []
        if j < last_hop:
            coming = [lax.ppermute(up, "rows", ahead), lax.ppermute(down, "rows", back)]
        elif j == last_hop:
            coming = [lax.ppermute(up, "rows", ahead)]
        chunks = [[piece, swap(piece, "vocab", vocab_count, 1)] for piece in arrived]
        held, acc, *rest = stage(planned(j), weight, table, rules, held, acc, chunks)
        if coming:
            arrived, held, acc = lax.optimization_barrier((coming, held, acc))
            up, down = arrived[0], arrived[-1]

    logits, lse = rest
    count = rows_count * vocab_count
    sent = jnp.broadcast_to(lse[None], (count, 1, all_rows))
    parts = lax.all_to_all(sent, ("rows", "vocab"), 0, 0, tiled=True)
    top = jnp.max(parts, axis=0)
    lse = top + jnp.log(jnp.sum(jnp.exp(parts - top), axis=0))
    log_probs = jnp.where(logits > reachable, logits - lse, 0.0)
    return log_probs.T, lse.reshape(all_rows)


def solution(mesh):
    placed = (
        P("vocab", "rows"),
        P("vocab"),
        P(None, ("rows", "vocab")),
        P(None, ("rows", "vocab")),
    )
    return jax.shard_map(
        functools.partial(local, mesh.shape["rows"], mesh.shape["vocab"]),
        mesh=mesh,
        in_specs=placed,
        out_specs=(P(None, ("rows", "vocab")), P()),
        check_vma=False,
    )
```

```python
import functools

import jax
import jax.numpy as jnp
from jax import lax
from jax.experimental import pallas as pl
from jax.experimental.pallas import tpu as pltpu
from jax.sharding import PartitionSpec as P

lowest = -1e30
reachable = -1e29


def ring_order(size):
    return list(range(0, size, 2)) + list(range(1, size, 2))[::-1]


def swap(x, axis, size, distance):
    return lax.ppermute(x, axis, [(i, i ^ distance) for i in range(size)])


def row_tile(columns):
    fits = [t for t in range(16, 529, 16) if columns % t == 0]
    return max(fits) if fits else columns


def ring_place(offset, count):
    here = lax.axis_index("rows")
    half = here // 2
    spot = jnp.where(here % 2 == 0, half, count - 1 - half)
    spot = lax.rem(spot + offset + count, count)
    return jnp.where(spot < count // 2, 2 * spot, 2 * (count - 1 - spot) + 1)


def stage_kernel(plan, *refs):
    rows_count, depth, columns, all_rows = plan["sizes"]
    refs = list(refs)
    take = lambda n: [refs.pop(0) for _ in range(n)]
    (weight,) = take(1)
    if plan["last"]:
        table_in, near, far = take(3)
    take(1 if plan["number"] > 1 else 0)
    held = take(plan["compute"])
    rows = take(plan["compute"])
    acc = take(1)[0] if rows else None
    loaded = take(len(plan["load"]))
    if plan["last"]:
        lse, turned, sems, table = take(4)
    else:
        turned, sems = take(2)

    tile = row_tile(columns)
    spans = [pl.ds(t * tile, tile) for t in range(columns // tile)]
    copies = []

    def begin(source, target):
        copies.append(pltpu.make_async_copy(source, target, sems.at[len(copies)]))
        copies[-1].start()

    for offset, target in zip(plan["load"], loaded):
        at = pl.multiple_of(ring_place(offset, rows_count) * depth, depth)
        for span in spans:
            begin(weight.at[span, pl.ds(at, depth)], target.at[span, :])
    if plan["last"]:
        for span in spans:
            begin(table_in.at[span, :], table.at[span, :])

    for c, ref in enumerate(rows):
        turned[c] = ref[...].astype(jnp.float32).T.astype(jnp.bfloat16)
    if plan["last"]:
        half = plan["vocab_count"] // 2
        block = all_rows // plan["vocab_count"]
        vocab_at = lax.axis_index("vocab")
        owner = lax.broadcasted_iota(jnp.int32, (1, all_rows), 1) // block
        wanted = jnp.zeros((1, all_rows), jnp.int32)
        for other, ref in enumerate((near, far)):
            for j in range(half):
                part = jnp.tile(ref[:, j * block : (j + 1) * block], (1, plan["vocab_count"]))
                wanted = jnp.where(owner == (vocab_at ^ (2 * j + other)), part, wanted)
        state = lax.broadcasted_iota(jnp.int32, (table.shape[1], all_rows), 0)
        marks = (state == wanted).astype(jnp.float32).astype(jnp.bfloat16)
    for span in spans if rows else []:
        total = None if plan["number"] == 1 else acc[span, :]
        for c, ref in enumerate(held):
            term = jnp.dot(ref[span, :], turned[c], preferred_element_type=jnp.float32)
            total = term if total is None else total + term
        acc[span, :] = total

    for copy in copies:
        copy.wait()

    if plan["last"]:
        peak = jnp.full((1, all_rows), lowest, jnp.float32)
        exps = jnp.zeros((1, all_rows), jnp.float32)
        for span in spans:
            rules = table[span, :].astype(jnp.float32).astype(jnp.bfloat16)
            allowed = jnp.dot(rules, marks, preferred_element_type=jnp.float32) > 0.5
            total = jnp.where(allowed, acc[span, :], lowest)
            new_peak = jnp.maximum(peak, jnp.max(total, axis=0, keepdims=True))
            terms = jnp.where(allowed, jnp.exp(total - new_peak), 0.0)
            exps = exps * jnp.exp(peak - new_peak) + jnp.sum(terms, axis=0, keepdims=True)
            peak = new_peak
            acc[span, :] = total
        lse[...] = jnp.where(exps > 0.0, peak + jnp.log(exps), lowest)


def stage(plan, weight, table, states, acc, held, rows):
    rows_count, depth, columns, all_rows = plan["sizes"]
    vmem = pl.BlockSpec(memory_space=pltpu.VMEM)
    keep = lambda x: pltpu.with_memory_space_constraint(x, pltpu.VMEM)
    args, specs, out, alias = [weight], [pl.BlockSpec(memory_space=pl.ANY)], [], {}
    if plan["last"]:
        args.append(pltpu.with_memory_space_constraint(table, pltpu.HBM))
        specs.append(pl.BlockSpec(memory_space=pltpu.HBM))
    if plan["last"]:
        args += states
    if acc is not None:
        alias[len(args)] = 0
        args.append(keep(acc))
    args += [keep(x) for x in held] + rows
    specs += [vmem] * (len(args) - len(specs))
    if rows:
        out.append(pltpu.VMEM((columns, all_rows), jnp.float32))
    out += [pltpu.VMEM((columns, depth), jnp.bfloat16)] * len(plan["load"])
    if plan["last"]:
        out.append(jax.ShapeDtypeStruct((1, all_rows), jnp.float32))
    count = max(1, len(plan["load"])) * (columns // row_tile(columns))
    scratch = [
        pltpu.VMEM((max(1, len(rows)), depth, all_rows), jnp.bfloat16),
        pltpu.SemaphoreType.DMA((count,)),
    ]
    if plan["last"]:
        scratch.append(pltpu.VMEM(table.shape, jnp.int32))
    return pl.pallas_call(
        functools.partial(stage_kernel, plan),
        in_specs=specs,
        out_shape=out,
        out_specs=[vmem] * len(out),
        input_output_aliases=alias,
        scratch_shapes=scratch,
        compiler_params=pltpu.CompilerParams(vmem_limit_bytes=(14 if plan["last"] else 2) * 2**20),
        cost_estimate=pl.CostEstimate(
            flops=2 * all_rows * depth * columns * plan["compute"],
            bytes_accessed=2 * columns * depth * len(plan["load"]),
            transcendentals=all_rows * columns * plan["last"],
        ),
    )(*args)


def join_kernel(vocab_count, *refs):
    pieces, states = refs[:vocab_count], refs[vocab_count:-2]
    rows, near = refs[-2:]
    block = pieces[0].shape[0]
    vocab_at = lax.axis_index("vocab")
    for d, ref in enumerate(pieces):
        rows[pl.ds(pl.multiple_of((vocab_at ^ d) * block, block), block), :] = ref[...]
    width = near.shape[1]
    owner = lax.broadcasted_iota(jnp.int32, (1, width), 1) // block
    joined = jnp.zeros((1, width), jnp.int32)
    for j, ref in enumerate(states):
        joined = jnp.where(owner == j, jnp.tile(ref[...], (1, width // block)), joined)
    near[...] = joined


def join(pieces, states):
    block, depth = pieces[0].shape
    width = -(-block * len(states) // 128) * 128
    vmem = pl.BlockSpec(memory_space=pltpu.VMEM)
    return pl.pallas_call(
        functools.partial(join_kernel, len(pieces)),
        in_specs=[vmem] * (len(pieces) + len(states)),
        out_specs=[vmem] * 2,
        out_shape=[
            jax.ShapeDtypeStruct((block * len(pieces), depth), jnp.bfloat16),
            jax.ShapeDtypeStruct((1, width), jnp.int32),
        ],
        compiler_params=pltpu.CompilerParams(vmem_limit_bytes=4 * 2**20),
    )(*pieces, *states)


def local(rows_count, vocab_count, hidden_rows, row_states, head_weight, grammar_table):
    block, depth = hidden_rows.shape
    columns = head_weight.shape[1]
    all_rows = block * vocab_count
    weight, table = head_weight.T, grammar_table.T

    row_states = row_states.reshape(1, block)
    pieces = [hidden_rows] + [swap(hidden_rows, "vocab", vocab_count, d) for d in range(1, vocab_count)]
    states = [row_states] + [swap(row_states, "vocab", vocab_count, 2 * d) for d in range(1, vocab_count // 2)]
    last_hop = rows_count // 2
    offsets = [0] + [s * j for j in range(1, last_hop) for s in (-1, 1)] + [last_hop]
    hops = [[0]] + [[2 * j - 1, 2 * j] for j in range(1, last_hop)] + [[rows_count - 1]]

    def planned(j):
        return dict(
            number=j,
            vocab_count=vocab_count,
            sizes=(rows_count, depth, columns, all_rows),
            load=[offsets[c] for c in hops[j]] if j <= last_hop else [],
            compute=len(hops[j - 1]) if j else 0,
            last=j > last_hop,
        )

    held = stage(planned(0), weight, table, None, None, [], [])
    pieces, states, held = lax.optimization_barrier((pieces, states, held))
    own, near = join(pieces, states)
    states = [near, swap(near, "vocab", vocab_count, 1)]

    order = ring_order(rows_count)
    ahead = [(order[i], order[(i + 1) % rows_count]) for i in range(rows_count)]
    back = [(b, a) for a, b in ahead]
    acc = None
    arrived = [own]
    for j in range(1, last_hop + 2):
        coming = []
        if j < last_hop:
            coming = [lax.ppermute(arrived[0], "rows", ahead), lax.ppermute(arrived[-1], "rows", back)]
        elif j == last_hop:
            coming = [lax.ppermute(arrived[0], "rows", ahead)]
        acc, *held = stage(planned(j), weight, table, states, acc, held, arrived)
        if coming:
            arrived, acc, held = lax.optimization_barrier((coming, acc, held))

    (lse,) = held
    count = rows_count * vocab_count
    sent = jnp.broadcast_to(lse[None], (count, 1, all_rows))
    parts = lax.all_to_all(sent, ("rows", "vocab"), 0, 0, tiled=True)
    top = jnp.max(parts, axis=0)
    lse = top + jnp.log(jnp.sum(jnp.exp(parts - top), axis=0))
    log_probs = jnp.where(acc > reachable, acc - lse, 0.0)
    return log_probs.T, lse.reshape(all_rows)


def solution(mesh):
    placed = (
        P("vocab", "rows"),
        P("vocab"),
        P(None, ("rows", "vocab")),
        P(None, ("rows", "vocab")),
    )
    return jax.shard_map(
        functools.partial(local, mesh.shape["rows"], mesh.shape["vocab"]),
        mesh=mesh,
        in_specs=placed,
        out_specs=(P(None, ("rows", "vocab")), P()),
        check_vma=False,
    )
```

```python
import functools

import jax
import jax.numpy as jnp
from jax import lax
from jax.experimental import pallas as pl
from jax.experimental.pallas import tpu as pltpu
from jax.sharding import PartitionSpec as P

lowest = -1e30
reachable = -1e29
slots = 4
raw_slots = 5


def ring_order(size):
    return list(range(0, size, 2)) + list(range(1, size, 2))[::-1]


def swap(x, axis, size, distance):
    return lax.ppermute(x, axis, [(i, i ^ distance) for i in range(size)])


def row_tile(columns):
    fits = [t for t in range(16, 529, 16) if columns % t == 0]
    return max(fits) if fits else columns


def up_to(size, step):
    return -(-size // step) * step


def ring_place(offset, count):
    here = lax.axis_index("rows")
    half = here // 2
    spot = jnp.where(here % 2 == 0, half, count - 1 - half)
    spot = lax.rem(spot + offset + count, count)
    return jnp.where(spot < count // 2, 2 * spot, 2 * (count - 1 - spot) + 1)


def stage_kernel(plan, *refs):
    rows_count, block, depth, columns, all_rows = plan["sizes"]
    half = plan["vocab_count"] // 2
    refs = list(refs)
    take = lambda n: [refs.pop(0) for _ in range(n)]
    (weight,) = take(1)
    if plan["load_table"]:
        (table_in,) = take(1)
    else:
        take(1)
    if plan["first"]:
        (rules_in,) = take(1)
    elif plan["compute"]:
        take(1)
    chunks = [(slot, take(2)) for slot in plan["compute"]]
    (held,) = take(1)
    acc = take(1)[0] if plan["compute"] else None
    lse = take(1)[0] if plan["last"] else None
    if plan["compute"]:
        hidden, turned, marks, sems = take(4)
    else:
        rules_out, raw, raw_sems, sems = take(4)

    tile = row_tile(columns)
    tiles = columns // tile
    copies = []
    for offset, slot in plan["load"]:
        at = pl.multiple_of(ring_place(offset, rows_count) * depth, depth)
        for t in range(tiles):
            span = pl.ds(t * tile, tile)
            copies.append((weight.at[span, pl.ds(at, depth)], held.at[slot, span, :]))
    copies = [pltpu.make_async_copy(a, b, sems.at[n]) for n, (a, b) in enumerate(copies)]
    if plan["compute"]:
        for copy in copies:
            copy.start()
    else:
        raw_copies = []
        for t in range(tiles):
            span = pl.ds(t * tile, tile)
            raw_copies.append(pltpu.make_async_copy(table_in.at[span, :], raw.at[t % raw_slots], raw_sems.at[t]))
        for copy in raw_copies[:raw_slots]:
            copy.start()
        for t in range(tiles):
            raw_copies[t].wait()
            copies[t].start()
            rules_out[pl.ds(t * tile, tile), :] = raw[t % raw_slots].astype(jnp.float32).astype(jnp.bfloat16)
            if t + raw_slots < tiles:
                raw_copies[t + raw_slots].start()

    if plan["compute"]:
        vocab_at = lax.axis_index("vocab")
        for c, (_, pieces) in enumerate(chunks):
            for other, ref in enumerate(pieces):
                for j in range(half):
                    owner = vocab_at ^ (2 * j + other)
                    at = pl.multiple_of(owner * block, block)
                    hidden[pl.ds(at, block), :] = ref[j * block : (j + 1) * block, :]
            turned[c] = hidden[...].astype(jnp.float32).T.astype(jnp.bfloat16)
        if plan["first"]:
            state_count = rules_in.shape[1]
            owner = lax.broadcasted_iota(jnp.int32, (1, all_rows), 1) // block
            wanted = jnp.zeros((1, all_rows), jnp.float32)
            for other, ref in enumerate(chunks[0][1]):
                digits = ref[half * block :, : up_to(half * block, 128)].astype(jnp.float32)
                states = digits[0:1] * 256.0 + digits[1:2]
                for j in range(half):
                    part = jnp.tile(states[:, j * block : (j + 1) * block], (1, all_rows // block))
                    wanted = jnp.where(owner == (vocab_at ^ (2 * j + other)), part, wanted)
            state = lax.broadcasted_iota(jnp.int32, (state_count, all_rows), 0).astype(jnp.float32)
            marks[...] = (state == wanted).astype(jnp.float32).astype(jnp.bfloat16)

        def work(t, carry):
            span = pl.ds(pl.multiple_of(t * tile, tile), tile) if tiles > 1 else slice(None)
            if plan["first"]:
                allowed = jnp.dot(rules_in[span, :], marks[...], preferred_element_type=jnp.float32) > 0.5
                total = jnp.where(allowed, 0.0, lowest)
            else:
                total = acc[span, :]
            for c, (slot, _) in enumerate(chunks):
                total += jnp.dot(held[slot, span, :], turned[c], preferred_element_type=jnp.float32)
            acc[span, :] = total
            if plan["last"]:
                peak, exps = carry
                new_peak = jnp.maximum(peak, jnp.max(total, axis=0, keepdims=True))
                terms = jnp.where(total > reachable, jnp.exp(total - new_peak), 0.0)
                exps = exps * jnp.exp(peak - new_peak) + jnp.sum(terms, axis=0, keepdims=True)
                return new_peak, exps
            return carry

        start = ()
        if plan["last"]:
            start = (jnp.full((1, all_rows), lowest, jnp.float32), jnp.zeros((1, all_rows), jnp.float32))
        done = lax.fori_loop(0, tiles, work, start, unroll=True)
        if plan["last"]:
            peak, exps = done
            lse[...] = jnp.where(exps > 0.0, peak + jnp.log(exps), lowest)

    for copy in copies:
        copy.wait()


def stage(plan, weight, table, rules, held, acc, chunks):
    rows_count, block, depth, columns, all_rows = plan["sizes"]
    vmem = pl.BlockSpec(memory_space=pltpu.VMEM)
    keep = lambda x: pltpu.with_memory_space_constraint(x, pltpu.VMEM)
    args, specs, out, alias = [weight], [pl.BlockSpec(memory_space=pl.ANY)], [], {}
    state_count = table.shape[1]
    if plan["load_table"]:
        args.append(pltpu.with_memory_space_constraint(table, pltpu.HBM))
        specs.append(pl.BlockSpec(memory_space=pltpu.HBM))
    else:
        alias[len(args)] = 0
        args.append(keep(held))
        specs.append(vmem)
    if plan["first"]:
        args.append(keep(rules))
        specs.append(vmem)
    elif plan["compute"]:
        alias[len(args)] = 1
        args.append(keep(acc))
        specs.append(vmem)
    args += [p for pieces in chunks for p in pieces]
    specs += [vmem] * sum(len(pieces) for pieces in chunks)
    out.append(pltpu.VMEM((slots, columns, depth), jnp.bfloat16))
    if plan["compute"]:
        out.append(pltpu.VMEM((columns, all_rows), jnp.float32))
    if plan["last"]:
        out.append(jax.ShapeDtypeStruct((1, all_rows), jnp.float32))
    tile = row_tile(columns)
    tiles = columns // tile
    sems = pltpu.SemaphoreType.DMA((max(1, tiles * len(plan["load"])),))
    if plan["compute"]:
        scratch = [
            pltpu.VMEM((all_rows, depth), jnp.bfloat16),
            pltpu.VMEM((len(plan["compute"]), depth, all_rows), jnp.bfloat16),
            pltpu.VMEM((state_count, all_rows), jnp.bfloat16),
            sems,
        ]
    else:
        out.append(pltpu.VMEM((columns, state_count), jnp.bfloat16))
        scratch = [
            pltpu.VMEM((raw_slots, tile, state_count), jnp.int32),
            pltpu.SemaphoreType.DMA((tiles,)),
            sems,
        ]
    moved = 2 * columns * depth * len(plan["load"]) + 4 * columns * state_count * plan["load_table"]
    return pl.pallas_call(
        functools.partial(stage_kernel, plan),
        in_specs=specs,
        out_shape=out,
        out_specs=[vmem] * len(out),
        input_output_aliases=alias,
        scratch_shapes=scratch,
        compiler_params=pltpu.CompilerParams(vmem_limit_bytes=7 * 2**20),
        cost_estimate=pl.CostEstimate(
            flops=2 * all_rows * depth * columns * len(plan["compute"]),
            bytes_accessed=moved,
            transcendentals=all_rows * columns * plan["last"],
        ),
    )(*args)


def join_kernel(half, *refs):
    pieces, states, (plain, marked) = refs[:half], refs[half : 2 * half], refs[2 * half :]
    block = pieces[0].shape[0]
    for j, ref in enumerate(pieces):
        plain[j * block : (j + 1) * block, :] = ref[...]
        marked[j * block : (j + 1) * block, :] = ref[...]
    width = up_to(half * block, 128)
    owner = lax.broadcasted_iota(jnp.int32, (1, width), 1) // block
    joined = jnp.zeros((1, width), jnp.int32)
    for j, ref in enumerate(states):
        joined = jnp.where(owner == j, jnp.tile(ref[...], (1, width // block)), joined)
    digit = lax.broadcasted_iota(jnp.int32, (16, width), 0)
    digits = jnp.where(digit == 0, joined // 256, jnp.where(digit == 1, joined % 256, 0))
    marked[half * block :, :width] = digits.astype(jnp.float32).astype(jnp.bfloat16)


def join(pieces, states):
    block, depth = pieces[0].shape
    rows = block * len(pieces)
    vmem = pl.BlockSpec(memory_space=pltpu.VMEM)
    return pl.pallas_call(
        functools.partial(join_kernel, len(pieces)),
        in_specs=[vmem] * (2 * len(pieces)),
        out_specs=[vmem] * 2,
        out_shape=[
            jax.ShapeDtypeStruct((rows, depth), jnp.bfloat16),
            jax.ShapeDtypeStruct((rows + 16, depth), jnp.bfloat16),
        ],
        compiler_params=pltpu.CompilerParams(vmem_limit_bytes=4 * 2**20),
    )(*pieces, *states)


def local(rows_count, vocab_count, hidden_rows, row_states, head_weight, grammar_table):
    block, depth = hidden_rows.shape
    columns = head_weight.shape[1]
    half = vocab_count // 2
    all_rows = block * vocab_count
    weight, table = head_weight.T, grammar_table.T

    row_states = row_states.reshape(1, block)
    shared = lambda x: [x] + [swap(x, "vocab", vocab_count, 2 * d) for d in range(1, half)]
    pieces, states = shared(hidden_rows), shared(row_states)
    plan = dict(
        vocab_count=vocab_count,
        sizes=(rows_count, block, depth, columns, all_rows),
        load=[(0, 0)],
        compute=[],
        load_table=True,
        first=False,
        last=False,
    )
    held, rules = stage(plan, weight, table, None, None, None, [])
    pieces, states, held, rules = lax.optimization_barrier((pieces, states, held, rules))
    own, marked = join(pieces, states)

    order = ring_order(rows_count)
    ahead = [(order[i], order[(i + 1) % rows_count]) for i in range(rows_count)]
    back = [(b, a) for a, b in ahead]
    last_hop = rows_count // 2
    acc, load, used = None, plan["load"], 1
    arrived = [(0, marked)]
    up = down = own
    for j in range(1, last_hop + 2):
        coming = []
        if j < last_hop:
            coming = [(-j, lax.ppermute(up, "rows", ahead)), (j, lax.ppermute(down, "rows", back))]
        elif j == last_hop:
            coming = [(j, lax.ppermute(up, "rows", ahead))]
        compute = [slot for _, slot in load]
        chunks = [[piece, swap(piece, "vocab", vocab_count, 1)] for _, piece in arrived]
        load = [(offset, (used + i) % slots) for i, (offset, _) in enumerate(coming)]
        used += len(load)
        plan = dict(
            vocab_count=vocab_count,
            sizes=(rows_count, block, depth, columns, all_rows),
            load=load,
            compute=compute,
            load_table=False,
            first=j == 1,
            last=j > last_hop,
        )
        res = list(stage(plan, weight, table, rules, held, acc, chunks))
        held, acc = res[:2]
        if plan["last"]:
            lse = res[2]
        else:
            pieces, held, acc = lax.optimization_barrier(([p for _, p in coming], held, acc))
            arrived = [(offset, p) for (offset, _), p in zip(coming, pieces)]
            up, down = pieces[0], pieces[-1]

    count = rows_count * vocab_count
    sent = jnp.broadcast_to(lse[None], (count, 1, all_rows))
    parts = lax.all_to_all(sent, ("rows", "vocab"), 0, 0, tiled=True)
    top = jnp.max(parts, axis=0)
    lse = top + jnp.log(jnp.sum(jnp.exp(parts - top), axis=0))
    log_probs = jnp.where(acc > reachable, acc - lse, 0.0)
    return log_probs.T, lse.reshape(all_rows)


def solution(mesh):
    placed = (
        P("vocab", "rows"),
        P("vocab"),
        P(None, ("rows", "vocab")),
        P(None, ("rows", "vocab")),
    )
    return jax.shard_map(
        functools.partial(local, mesh.shape["rows"], mesh.shape["vocab"]),
        mesh=mesh,
        in_specs=placed,
        out_specs=(P(None, ("rows", "vocab")), P()),
        check_vma=False,
    )
```

```python
import functools

import jax
import jax.numpy as jnp
from jax import lax
from jax.experimental import pallas as pl
from jax.experimental.pallas import tpu as pltpu
from jax.sharding import PartitionSpec as P

lowest = -1e30
reachable = -1e29
slots = 4
raw_slots = 5


def ring_order(size):
    return list(range(0, size, 2)) + list(range(1, size, 2))[::-1]


def swap(x, axis, size, distance):
    return lax.ppermute(x, axis, [(i, i ^ distance) for i in range(size)])


def row_tile(columns):
    fits = [t for t in range(16, 529, 16) if columns % t == 0]
    return max(fits) if fits else columns


def ring_place(offset, count):
    here = lax.axis_index("rows")
    half = here // 2
    spot = jnp.where(here % 2 == 0, half, count - 1 - half)
    spot = lax.rem(spot + offset + count, count)
    return jnp.where(spot < count // 2, 2 * spot, 2 * (count - 1 - spot) + 1)


def stage_kernel(plan, *refs):
    rows_count, block, depth, columns, all_rows = plan["sizes"]
    half = plan["vocab_count"] // 2
    refs = list(refs)
    take = lambda n: [refs.pop(0) for _ in range(n)]
    (weight,) = take(1)
    if plan["load_table"]:
        (table_in,) = take(1)
    else:
        take(1)
    if plan["first"]:
        rules_in, near, far = take(3)
    elif plan["compute"]:
        take(1)
    chunks = [(slot, take(1)[0]) for slot in plan["compute"]]
    (held,) = take(1)
    acc = take(1)[0] if plan["compute"] else None
    lse = take(1)[0] if plan["last"] else None
    if plan["compute"]:
        turned, marks, sems = take(3)
    else:
        rules_out, raw, raw_sems, sems = take(4)

    tile = row_tile(columns)
    tiles = columns // tile
    copies = []
    for offset, slot in plan["load"]:
        at = pl.multiple_of(ring_place(offset, rows_count) * depth, depth)
        for t in range(tiles):
            span = pl.ds(t * tile, tile)
            copies.append((weight.at[span, pl.ds(at, depth)], held.at[slot, span, :]))
    copies = [pltpu.make_async_copy(a, b, sems.at[n]) for n, (a, b) in enumerate(copies)]
    if plan["compute"]:
        for copy in copies:
            copy.start()
    else:
        raw_copies = []
        for t in range(tiles):
            span = pl.ds(t * tile, tile)
            raw_copies.append(pltpu.make_async_copy(table_in.at[span, :], raw.at[t % raw_slots], raw_sems.at[t]))
        for copy in raw_copies[:raw_slots]:
            copy.start()
        for t in range(tiles):
            raw_copies[t].wait()
            copies[t].start()
            rules_out[pl.ds(t * tile, tile), :] = raw[t % raw_slots].astype(jnp.float32).astype(jnp.bfloat16)
            if t + raw_slots < tiles:
                raw_copies[t + raw_slots].start()

    if plan["compute"]:
        for c, (_, ref) in enumerate(chunks):
            turned[c] = ref[...].astype(jnp.float32).T.astype(jnp.bfloat16)
        if plan["first"]:
            state_count = rules_in.shape[1]
            owner = lax.broadcasted_iota(jnp.int32, (1, all_rows), 1) // block
            wanted = jnp.zeros((1, all_rows), jnp.int32)
            vocab_at = lax.axis_index("vocab")
            for other, ref in enumerate((near, far)):
                for j in range(half):
                    part = jnp.tile(ref[:, j * block : (j + 1) * block], (1, all_rows // block))
                    wanted = jnp.where(owner == (vocab_at ^ (2 * j + other)), part, wanted)
            state = lax.broadcasted_iota(jnp.int32, (state_count, all_rows), 0)
            marks[...] = (state == wanted).astype(jnp.float32).astype(jnp.bfloat16)

        def work(t, carry):
            span = pl.ds(pl.multiple_of(t * tile, tile), tile) if tiles > 1 else slice(None)
            if plan["first"]:
                allowed = jnp.dot(rules_in[span, :], marks[...], preferred_element_type=jnp.float32) > 0.5
                total = jnp.where(allowed, 0.0, lowest)
            else:
                total = acc[span, :]
            for c, (slot, _) in enumerate(chunks):
                total += jnp.dot(held[slot, span, :], turned[c], preferred_element_type=jnp.float32)
            acc[span, :] = total
            if plan["last"]:
                peak, exps = carry
                new_peak = jnp.maximum(peak, jnp.max(total, axis=0, keepdims=True))
                terms = jnp.where(total > reachable, jnp.exp(total - new_peak), 0.0)
                exps = exps * jnp.exp(peak - new_peak) + jnp.sum(terms, axis=0, keepdims=True)
                return new_peak, exps
            return carry

        start = ()
        if plan["last"]:
            start = (jnp.full((1, all_rows), lowest, jnp.float32), jnp.zeros((1, all_rows), jnp.float32))
        done = lax.fori_loop(0, tiles, work, start, unroll=True)
        if plan["last"]:
            peak, exps = done
            lse[...] = jnp.where(exps > 0.0, peak + jnp.log(exps), lowest)

    for copy in copies:
        copy.wait()


def stage(plan, weight, table, rules, states, held, acc, rows):
    rows_count, block, depth, columns, all_rows = plan["sizes"]
    vmem = pl.BlockSpec(memory_space=pltpu.VMEM)
    keep = lambda x: pltpu.with_memory_space_constraint(x, pltpu.VMEM)
    args, specs, out, alias = [weight], [pl.BlockSpec(memory_space=pl.ANY)], [], {}
    state_count = table.shape[1]
    if plan["load_table"]:
        args.append(pltpu.with_memory_space_constraint(table, pltpu.HBM))
        specs.append(pl.BlockSpec(memory_space=pltpu.HBM))
    else:
        alias[len(args)] = 0
        args.append(keep(held))
        specs.append(vmem)
    if plan["first"]:
        args += [keep(rules), *states]
        specs += [vmem] * 3
    elif plan["compute"]:
        alias[len(args)] = 1
        args.append(keep(acc))
        specs.append(vmem)
    args += rows
    specs += [vmem] * len(rows)
    out.append(pltpu.VMEM((slots, columns, depth), jnp.bfloat16))
    if plan["compute"]:
        out.append(pltpu.VMEM((columns, all_rows), jnp.float32))
    if plan["last"]:
        out.append(jax.ShapeDtypeStruct((1, all_rows), jnp.float32))
    tile = row_tile(columns)
    tiles = columns // tile
    sems = pltpu.SemaphoreType.DMA((max(1, tiles * len(plan["load"])),))
    if plan["compute"]:
        scratch = [
            pltpu.VMEM((len(plan["compute"]), depth, all_rows), jnp.bfloat16),
            pltpu.VMEM((state_count, all_rows), jnp.bfloat16),
            sems,
        ]
    else:
        out.append(pltpu.VMEM((columns, state_count), jnp.bfloat16))
        scratch = [
            pltpu.VMEM((raw_slots, tile, state_count), jnp.int32),
            pltpu.SemaphoreType.DMA((tiles,)),
            sems,
        ]
    moved = 2 * columns * depth * len(plan["load"]) + 4 * columns * state_count * plan["load_table"]
    return pl.pallas_call(
        functools.partial(stage_kernel, plan),
        in_specs=specs,
        out_shape=out,
        out_specs=[vmem] * len(out),
        input_output_aliases=alias,
        scratch_shapes=scratch,
        compiler_params=pltpu.CompilerParams(vmem_limit_bytes=7 * 2**20),
        cost_estimate=pl.CostEstimate(
            flops=2 * all_rows * depth * columns * len(plan["compute"]),
            bytes_accessed=moved,
            transcendentals=all_rows * columns * plan["last"],
        ),
    )(*args)


def join_kernel(vocab_count, *refs):
    pieces, states = refs[:vocab_count], refs[vocab_count:-2]
    rows, near = refs[-2:]
    block = pieces[0].shape[0]
    vocab_at = lax.axis_index("vocab")
    for d, ref in enumerate(pieces):
        rows[pl.ds(pl.multiple_of((vocab_at ^ d) * block, block), block), :] = ref[...]
    width = near.shape[1]
    owner = lax.broadcasted_iota(jnp.int32, (1, width), 1) // block
    joined = jnp.zeros((1, width), jnp.int32)
    for j, ref in enumerate(states):
        joined = jnp.where(owner == j, jnp.tile(ref[...], (1, width // block)), joined)
    near[...] = joined


def join(pieces, states):
    block, depth = pieces[0].shape
    width = -(-block * len(states) // 128) * 128
    vmem = pl.BlockSpec(memory_space=pltpu.VMEM)
    return pl.pallas_call(
        functools.partial(join_kernel, len(pieces)),
        in_specs=[vmem] * (len(pieces) + len(states)),
        out_specs=[vmem] * 2,
        out_shape=[
            jax.ShapeDtypeStruct((block * len(pieces), depth), jnp.bfloat16),
            jax.ShapeDtypeStruct((1, width), jnp.int32),
        ],
        compiler_params=pltpu.CompilerParams(vmem_limit_bytes=4 * 2**20),
    )(*pieces, *states)


def local(rows_count, vocab_count, hidden_rows, row_states, head_weight, grammar_table):
    block, depth = hidden_rows.shape
    columns = head_weight.shape[1]
    half = vocab_count // 2
    all_rows = block * vocab_count
    weight, table = head_weight.T, grammar_table.T

    row_states = row_states.reshape(1, block)
    pieces = [hidden_rows] + [swap(hidden_rows, "vocab", vocab_count, d) for d in range(1, vocab_count)]
    states = [row_states] + [swap(row_states, "vocab", vocab_count, 2 * d) for d in range(1, half)]
    plan = dict(
        vocab_count=vocab_count,
        sizes=(rows_count, block, depth, columns, all_rows),
        load=[(0, 0)],
        compute=[],
        load_table=True,
        first=False,
        last=False,
    )
    held, rules = stage(plan, weight, table, None, None, None, None, [])
    pieces, states, held, rules = lax.optimization_barrier((pieces, states, held, rules))
    own, near = join(pieces, states)
    states = [near, swap(near, "vocab", vocab_count, 1)]

    order = ring_order(rows_count)
    ahead = [(order[i], order[(i + 1) % rows_count]) for i in range(rows_count)]
    back = [(b, a) for a, b in ahead]
    last_hop = rows_count // 2
    acc, load, used = None, plan["load"], 1
    arrived = [(0, own)]
    up = down = own
    for j in range(1, last_hop + 2):
        coming = []
        if j < last_hop:
            coming = [(-j, lax.ppermute(up, "rows", ahead)), (j, lax.ppermute(down, "rows", back))]
        elif j == last_hop:
            coming = [(j, lax.ppermute(up, "rows", ahead))]
        compute = [slot for _, slot in load]
        rows = [piece for _, piece in arrived]
        load = [(offset, (used + i) % slots) for i, (offset, _) in enumerate(coming)]
        used += len(load)
        plan = dict(
            vocab_count=vocab_count,
            sizes=(rows_count, block, depth, columns, all_rows),
            load=load,
            compute=compute,
            load_table=False,
            first=j == 1,
            last=j > last_hop,
        )
        res = list(stage(plan, weight, table, rules, states, held, acc, rows))
        held, acc = res[:2]
        if plan["last"]:
            lse = res[2]
        else:
            pieces, held, acc = lax.optimization_barrier(([p for _, p in coming], held, acc))
            arrived = [(offset, p) for (offset, _), p in zip(coming, pieces)]
            up, down = pieces[0], pieces[-1]

    count = rows_count * vocab_count
    sent = jnp.broadcast_to(lse[None], (count, 1, all_rows))
    parts = lax.all_to_all(sent, ("rows", "vocab"), 0, 0, tiled=True)
    top = jnp.max(parts, axis=0)
    lse = top + jnp.log(jnp.sum(jnp.exp(parts - top), axis=0))
    log_probs = jnp.where(acc > reachable, acc - lse, 0.0)
    return log_probs.T, lse.reshape(all_rows)


def solution(mesh):
    placed = (
        P("vocab", "rows"),
        P("vocab"),
        P(None, ("rows", "vocab")),
        P(None, ("rows", "vocab")),
    )
    return jax.shard_map(
        functools.partial(local, mesh.shape["rows"], mesh.shape["vocab"]),
        mesh=mesh,
        in_specs=placed,
        out_specs=(P(None, ("rows", "vocab")), P()),
        check_vma=False,
    )
```

```python
import functools

import jax
import jax.numpy as jnp
from jax import lax
from jax.experimental import pallas as pl
from jax.experimental.pallas import tpu as pltpu
from jax.sharding import PartitionSpec as P

lowest = -1e30
reachable = -1e29
slots = 4
raw_slots = 5
wide = 512
NT = (((1,), (1,)), ((), ()))


def ring_order(size):
    return list(range(0, size, 2)) + list(range(1, size, 2))[::-1]


def swap(x, axis, size, distance):
    return lax.ppermute(x, axis, [(i, i ^ distance) for i in range(size)])


def row_tile(columns):
    fits = [t for t in range(16, 529, 16) if columns % t == 0]
    return max(fits) if fits else columns


def copy_spans(columns):
    size = columns // 3
    return [(0, columns)] if columns % 48 else [(t * size, size) for t in range(3)]


def ring_place(offset, count):
    here = lax.axis_index("rows")
    half = here // 2
    spot = jnp.where(here % 2 == 0, half, count - 1 - half)
    spot = lax.rem(spot + offset + count, count)
    return jnp.where(spot < count // 2, 2 * spot, 2 * (count - 1 - spot) + 1)


def stage_kernel(plan, *refs):
    rows_count, block, depth, columns, all_rows = plan["sizes"]
    refs = list(refs)
    take = lambda n: [refs.pop(0) for _ in range(n)]
    (weight,) = take(1)
    if plan["load_table"]:
        (table_in,) = take(1)
    else:
        take(1)
    if plan["first"]:
        states, rules_in = take(plan["vocab_count"]), take(1)[0]
    elif plan["compute"]:
        take(1)
    rows = take(len(plan["compute"]))
    (held,) = take(1)
    acc = take(1)[0] if plan["compute"] else None
    turned, lse = take(2) if plan["last"] else (None, None)
    if plan["compute"]:
        marks, sems = take(2)
    else:
        rules_out, raw, raw_sems, sems = take(4)

    copies = []
    for offset, slot in plan["load"]:
        at = pl.multiple_of(ring_place(offset, rows_count) * depth, depth)
        for begin, size in copy_spans(columns):
            span = pl.ds(begin, size)
            source = weight.at[span, pl.ds(at, depth)]
            copies.append(pltpu.make_async_copy(source, held.at[slot, span, :], sems.at[len(copies)]))
    if plan["compute"]:
        for copy in copies:
            copy.start()
    else:
        tile = row_tile(columns)
        tiles = columns // tile
        raw_copies = []
        for t in range(tiles):
            span = pl.ds(t * tile, tile)
            raw_copies.append(pltpu.make_async_copy(table_in.at[span, :], raw.at[t % raw_slots], raw_sems.at[t]))
        for copy in raw_copies[:raw_slots]:
            copy.start()
        for t in range(tiles):
            raw_copies[t].wait()
            if t < len(copies):
                copies[t].start()
            rules_out[pl.ds(t * tile, tile), :] = raw[t % raw_slots].astype(jnp.float32).astype(jnp.bfloat16)
            if t + raw_slots < tiles:
                raw_copies[t + raw_slots].start()
        for copy in copies[tiles:]:
            copy.start()

    if plan["compute"]:
        if plan["first"]:
            state_count = rules_in.shape[1]
            owner = lax.broadcasted_iota(jnp.int32, (1, all_rows), 1) // block
            wanted = jnp.zeros((1, all_rows), jnp.int32)
            vocab_at = lax.axis_index("vocab")
            for d, part in enumerate(states):
                wanted = jnp.where(owner == (vocab_at ^ d), jnp.tile(part[...], (1, all_rows // block)), wanted)
            state = lax.broadcasted_iota(jnp.int32, (state_count, all_rows), 0)
            marks[...] = (state == wanted).astype(jnp.float32).T.astype(jnp.bfloat16)

        def piece(begin, size, carry):
            span = pl.ds(begin, size)
            if plan["first"]:
                hits = lax.dot_general(marks[...], rules_in[span, :], NT, preferred_element_type=jnp.float32)
                total = jnp.where(hits > 0.5, 0.0, lowest)
            else:
                total = acc[:, span]
            for ref, slot in zip(rows, plan["compute"]):
                total += lax.dot_general(ref[...], held[slot, span, :], NT, preferred_element_type=jnp.float32)
            if not plan["last"]:
                acc[:, span] = total
                return carry
            turned[span, :] = total.T
            peak, exps = carry
            new_peak = jnp.maximum(peak, jnp.max(total, axis=1, keepdims=True))
            terms = jnp.where(total > reachable, jnp.exp(total - new_peak), 0.0)
            exps = exps * jnp.exp(peak - new_peak) + jnp.sum(terms, axis=1, keepdims=True)
            return new_peak, exps

        carry = ()
        if plan["last"]:
            carry = (jnp.full((all_rows, 1), lowest, jnp.float32), jnp.zeros((all_rows, 1), jnp.float32))
        whole = 0 if columns % 16 else columns // wide
        if whole:
            move = lambda t, c: piece(pl.multiple_of(t * wide, wide), wide, c)
            carry = lax.fori_loop(0, whole, move, carry, unroll=True)
        if columns > whole * wide:
            carry = piece(whole * wide, columns - whole * wide, carry)
        if plan["last"]:
            peak, exps = carry
            found = jnp.where(exps > 0.0, peak + jnp.log(exps), lowest)
            lse[...] = jnp.broadcast_to(found, (all_rows, 128)).T[0:1, :]

    for copy in copies:
        copy.wait()


def stage(plan, weight, table, rules, states, held, acc, rows):
    rows_count, block, depth, columns, all_rows = plan["sizes"]
    vmem = pl.BlockSpec(memory_space=pltpu.VMEM)
    keep = lambda x: pltpu.with_memory_space_constraint(x, pltpu.VMEM)
    args, specs, out, alias = [weight], [pl.BlockSpec(memory_space=pl.ANY)], [], {}
    state_count = table.shape[1]
    if plan["load_table"]:
        args.append(pltpu.with_memory_space_constraint(table, pltpu.HBM))
        specs.append(pl.BlockSpec(memory_space=pltpu.HBM))
    else:
        alias[len(args)] = 0
        args.append(keep(held))
        specs.append(vmem)
    if plan["first"]:
        args += [*states, keep(rules)]
        specs += [vmem] * (len(states) + 1)
    elif plan["compute"]:
        alias[len(args)] = 1
        args.append(keep(acc))
        specs.append(vmem)
    args += rows
    specs += [vmem] * len(rows)
    out.append(pltpu.VMEM((slots, columns, depth), jnp.bfloat16))
    if plan["compute"]:
        out.append(pltpu.VMEM((all_rows, -(-columns // 128) * 128), jnp.float32))
    if plan["last"]:
        out.append(pltpu.VMEM((columns, all_rows), jnp.float32))
        out.append(jax.ShapeDtypeStruct((1, all_rows), jnp.float32))
    tile = row_tile(columns)
    tiles = columns // tile
    sems = pltpu.SemaphoreType.DMA((max(1, len(copy_spans(columns)) * len(plan["load"])),))
    if plan["compute"]:
        scratch = [
            pltpu.VMEM((all_rows, state_count), jnp.bfloat16),
            sems,
        ]
    else:
        out.append(pltpu.VMEM((columns, state_count), jnp.bfloat16))
        scratch = [
            pltpu.VMEM((raw_slots, tile, state_count), jnp.int32),
            pltpu.SemaphoreType.DMA((tiles,)),
            sems,
        ]
    moved = 2 * columns * depth * len(plan["load"]) + 4 * columns * state_count * plan["load_table"]
    return pl.pallas_call(
        functools.partial(stage_kernel, plan),
        in_specs=specs,
        out_shape=out,
        out_specs=[vmem] * len(out),
        input_output_aliases=alias,
        scratch_shapes=scratch,
        compiler_params=pltpu.CompilerParams(vmem_limit_bytes=7 * 2**20),
        cost_estimate=pl.CostEstimate(
            flops=2 * all_rows * depth * columns * len(plan["compute"]),
            bytes_accessed=moved,
            transcendentals=all_rows * columns * plan["last"],
        ),
    )(*args)


def join_kernel(*refs):
    block = refs[0].shape[0]
    vocab_at = lax.axis_index("vocab")
    for d, ref in enumerate(refs[:-1]):
        refs[-1][pl.ds(pl.multiple_of((vocab_at ^ d) * block, block), block), :] = ref[...]


def join(pieces):
    block, depth = pieces[0].shape
    vmem = pl.BlockSpec(memory_space=pltpu.VMEM)
    return pl.pallas_call(
        join_kernel,
        in_specs=[vmem] * len(pieces),
        out_specs=vmem,
        out_shape=jax.ShapeDtypeStruct((block * len(pieces), depth), jnp.bfloat16),
        compiler_params=pltpu.CompilerParams(vmem_limit_bytes=4 * 2**20),
    )(*pieces)


def local(rows_count, vocab_count, hidden_rows, row_states, head_weight, grammar_table):
    block, depth = hidden_rows.shape
    columns = head_weight.shape[1]
    all_rows = block * vocab_count
    weight, table = head_weight.T, grammar_table.T

    row_states = row_states.reshape(1, block)
    pieces = [hidden_rows] + [swap(hidden_rows, "vocab", vocab_count, d) for d in range(1, vocab_count)]
    states = [row_states] + [swap(row_states, "vocab", vocab_count, d) for d in range(1, vocab_count)]
    plan = dict(
        vocab_count=vocab_count,
        sizes=(rows_count, block, depth, columns, all_rows),
        load=[(0, 0)],
        compute=[],
        load_table=True,
        first=False,
        last=False,
    )
    held, rules = stage(plan, weight, table, None, None, None, None, [])
    pieces, states, held, rules = lax.optimization_barrier((pieces, states, held, rules))
    own = join(pieces)

    order = ring_order(rows_count)
    ahead = [(order[i], order[(i + 1) % rows_count]) for i in range(rows_count)]
    back = [(b, a) for a, b in ahead]
    last_hop = rows_count // 2
    acc, load, used = None, plan["load"], 1
    arrived = [(0, own)]
    up = down = own
    for j in range(1, last_hop + 2):
        coming = []
        if j < last_hop:
            coming = [(-j, lax.ppermute(up, "rows", ahead)), (j, lax.ppermute(down, "rows", back))]
        elif j == last_hop:
            coming = [(j, lax.ppermute(up, "rows", ahead))]
        compute = [slot for _, slot in load]
        rows = [piece for _, piece in arrived]
        load = [(offset, (used + i) % slots) for i, (offset, _) in enumerate(coming)]
        used += len(load)
        plan = dict(
            vocab_count=vocab_count,
            sizes=(rows_count, block, depth, columns, all_rows),
            load=load,
            compute=compute,
            load_table=False,
            first=j == 1,
            last=j > last_hop,
        )
        res = list(stage(plan, weight, table, rules, states, held, acc, rows))
        held, acc = res[:2]
        if plan["last"]:
            logits, lse = res[2:]
        else:
            pieces, held, acc = lax.optimization_barrier(([p for _, p in coming], held, acc))
            arrived = [(offset, p) for (offset, _), p in zip(coming, pieces)]
            up, down = pieces[0], pieces[-1]

    count = rows_count * vocab_count
    sent = jnp.broadcast_to(lse[None], (count, 1, all_rows))
    parts = lax.all_to_all(sent, ("rows", "vocab"), 0, 0, tiled=True)
    top = jnp.max(parts, axis=0)
    lse = top + jnp.log(jnp.sum(jnp.exp(parts - top), axis=0))
    log_probs = jnp.where(logits > reachable, logits - lse, 0.0)
    return log_probs.T, lse.reshape(all_rows)


def solution(mesh):
    placed = (
        P("vocab", "rows"),
        P("vocab"),
        P(None, ("rows", "vocab")),
        P(None, ("rows", "vocab")),
    )
    return jax.shard_map(
        functools.partial(local, mesh.shape["rows"], mesh.shape["vocab"]),
        mesh=mesh,
        in_specs=placed,
        out_specs=(P(None, ("rows", "vocab")), P()),
        check_vma=False,
    )
```

```python
import functools

import jax
import jax.numpy as jnp
from jax import lax
from jax.experimental import pallas as pl
from jax.experimental.pallas import tpu as pltpu
from jax.sharding import PartitionSpec as P

lowest = -1e30
reachable = -1e29
slots = 4
raw_slots = 5


def ring_order(size):
    return list(range(0, size, 2)) + list(range(1, size, 2))[::-1]


def swap(x, axis, size, distance):
    return lax.ppermute(x, axis, [(i, i ^ distance) for i in range(size)])


def row_tile(columns):
    fits = [t for t in range(16, 529, 16) if columns % t == 0]
    return max(fits) if fits else columns


def ring_place(offset, count):
    here = lax.axis_index("rows")
    half = here // 2
    spot = jnp.where(here % 2 == 0, half, count - 1 - half)
    spot = lax.rem(spot + offset + count, count)
    return jnp.where(spot < count // 2, 2 * spot, 2 * (count - 1 - spot) + 1)


def stage_kernel(plan, *refs):
    rows_count, block, depth, columns, all_rows = plan["sizes"]
    half = plan["vocab_count"] // 2
    refs = list(refs)
    take = lambda n: [refs.pop(0) for _ in range(n)]
    (weight,) = take(1)
    if plan["load_table"]:
        (table_in,) = take(1)
    else:
        take(1)
    if plan["mask"]:
        rules_in, near, far = take(3)
    if plan["compute"] and not plan["first"]:
        take(1)
    chunks = [(slot, take(1)[0]) for slot in plan["compute"]]
    (held,) = take(1)
    acc = take(1)[0] if plan["compute"] else None
    lse = take(1)[0] if plan["last"] else None
    if plan["compute"]:
        turned, marks, sems = take(3)
    else:
        rules_out, raw, raw_sems, sems = take(4)

    tile = row_tile(columns)
    tiles = columns // tile
    copies = []
    for offset, slot in plan["load"]:
        at = pl.multiple_of(ring_place(offset, rows_count) * depth, depth)
        for t in range(tiles):
            span = pl.ds(t * tile, tile)
            copies.append((weight.at[span, pl.ds(at, depth)], held.at[slot, span, :]))
    copies = [pltpu.make_async_copy(a, b, sems.at[n]) for n, (a, b) in enumerate(copies)]
    if plan["compute"]:
        for copy in copies:
            copy.start()
    else:
        raw_copies = []
        for t in range(tiles):
            span = pl.ds(t * tile, tile)
            raw_copies.append(pltpu.make_async_copy(table_in.at[span, :], raw.at[t % raw_slots], raw_sems.at[t]))
        for copy in raw_copies[:raw_slots]:
            copy.start()
        for t in range(tiles):
            raw_copies[t].wait()
            copies[t].start()
            rules_out[pl.ds(t * tile, tile), :] = raw[t % raw_slots].astype(jnp.float32).astype(jnp.bfloat16)
            if t + raw_slots < tiles:
                raw_copies[t + raw_slots].start()

    if plan["compute"]:
        for c, (_, ref) in enumerate(chunks):
            turned[c] = ref[...].astype(jnp.float32).T.astype(jnp.bfloat16)
        if plan["mask"]:
            state_count = rules_in.shape[1]
            owner = lax.broadcasted_iota(jnp.int32, (1, all_rows), 1) // block
            wanted = jnp.zeros((1, all_rows), jnp.int32)
            vocab_at = lax.axis_index("vocab")
            for other, ref in enumerate((near, far)):
                for j in range(half):
                    part = jnp.tile(ref[:, j * block : (j + 1) * block], (1, all_rows // block))
                    wanted = jnp.where(owner == (vocab_at ^ (2 * j + other)), part, wanted)
            state = lax.broadcasted_iota(jnp.int32, (state_count, all_rows), 0)
            marks[...] = (state == wanted).astype(jnp.float32).astype(jnp.bfloat16)

        def work(t, carry):
            span = pl.ds(pl.multiple_of(t * tile, tile), tile) if tiles > 1 else slice(None)
            total = 0.0 if plan["first"] else acc[span, :]
            if plan["mask"]:
                allowed = jnp.dot(rules_in[span, :], marks[...], preferred_element_type=jnp.float32) > 0.5
                total = jnp.where(allowed, total, lowest)
            for c, (slot, _) in enumerate(chunks):
                total += jnp.dot(held[slot, span, :], turned[c], preferred_element_type=jnp.float32)
            acc[span, :] = total
            if plan["last"]:
                peak, exps = carry
                new_peak = jnp.maximum(peak, jnp.max(total, axis=0, keepdims=True))
                terms = jnp.where(total > reachable, jnp.exp(total - new_peak), 0.0)
                exps = exps * jnp.exp(peak - new_peak) + jnp.sum(terms, axis=0, keepdims=True)
                return new_peak, exps
            return carry

        start = ()
        if plan["last"]:
            start = (jnp.full((1, all_rows), lowest, jnp.float32), jnp.zeros((1, all_rows), jnp.float32))
        done = lax.fori_loop(0, tiles, work, start, unroll=True)
        if plan["last"]:
            peak, exps = done
            lse[...] = jnp.where(exps > 0.0, peak + jnp.log(exps), lowest)

    for copy in copies:
        copy.wait()


def stage(plan, weight, table, rules, states, held, acc, rows):
    rows_count, block, depth, columns, all_rows = plan["sizes"]
    vmem = pl.BlockSpec(memory_space=pltpu.VMEM)
    keep = lambda x: pltpu.with_memory_space_constraint(x, pltpu.VMEM)
    args, specs, out, alias = [weight], [pl.BlockSpec(memory_space=pl.ANY)], [], {}
    state_count = table.shape[1]
    if plan["load_table"]:
        args.append(pltpu.with_memory_space_constraint(table, pltpu.HBM))
        specs.append(pl.BlockSpec(memory_space=pltpu.HBM))
    else:
        alias[len(args)] = 0
        args.append(keep(held))
        specs.append(vmem)
    if plan["mask"]:
        args += [keep(rules), *states]
        specs += [vmem] * 3
    if plan["compute"] and not plan["first"]:
        alias[len(args)] = 1
        args.append(keep(acc))
        specs.append(vmem)
    args += rows
    specs += [vmem] * len(rows)
    out.append(pltpu.VMEM((slots, columns, depth), jnp.bfloat16))
    if plan["compute"]:
        out.append(pltpu.VMEM((columns, all_rows), jnp.float32))
    if plan["last"]:
        out.append(jax.ShapeDtypeStruct((1, all_rows), jnp.float32))
    tile = row_tile(columns)
    tiles = columns // tile
    sems = pltpu.SemaphoreType.DMA((max(1, tiles * len(plan["load"])),))
    if plan["compute"]:
        scratch = [
            pltpu.VMEM((len(plan["compute"]), depth, all_rows), jnp.bfloat16),
            pltpu.VMEM((state_count, all_rows), jnp.bfloat16),
            sems,
        ]
    else:
        out.append(pltpu.VMEM((columns, state_count), jnp.bfloat16))
        scratch = [
            pltpu.VMEM((raw_slots, tile, state_count), jnp.int32),
            pltpu.SemaphoreType.DMA((tiles,)),
            sems,
        ]
    moved = 2 * columns * depth * len(plan["load"]) + 4 * columns * state_count * plan["load_table"]
    return pl.pallas_call(
        functools.partial(stage_kernel, plan),
        in_specs=specs,
        out_shape=out,
        out_specs=[vmem] * len(out),
        input_output_aliases=alias,
        scratch_shapes=scratch,
        compiler_params=pltpu.CompilerParams(vmem_limit_bytes=7 * 2**20),
        cost_estimate=pl.CostEstimate(
            flops=2 * all_rows * depth * columns * len(plan["compute"]),
            bytes_accessed=moved,
            transcendentals=all_rows * columns * plan["last"],
        ),
    )(*args)


def join_kernel(vocab_count, *refs):
    pieces, states = refs[:vocab_count], refs[vocab_count:-2]
    rows, near = refs[-2:]
    block = pieces[0].shape[0]
    vocab_at = lax.axis_index("vocab")
    for d, ref in enumerate(pieces):
        rows[pl.ds(pl.multiple_of((vocab_at ^ d) * block, block), block), :] = ref[...]
    width = near.shape[1]
    owner = lax.broadcasted_iota(jnp.int32, (1, width), 1) // block
    joined = jnp.zeros((1, width), jnp.int32)
    for j, ref in enumerate(states):
        joined = jnp.where(owner == j, jnp.tile(ref[...], (1, width // block)), joined)
    near[...] = joined


def join(pieces, states):
    block, depth = pieces[0].shape
    width = -(-block * len(states) // 128) * 128
    vmem = pl.BlockSpec(memory_space=pltpu.VMEM)
    return pl.pallas_call(
        functools.partial(join_kernel, len(pieces)),
        in_specs=[vmem] * (len(pieces) + len(states)),
        out_specs=[vmem] * 2,
        out_shape=[
            jax.ShapeDtypeStruct((block * len(pieces), depth), jnp.bfloat16),
            jax.ShapeDtypeStruct((1, width), jnp.int32),
        ],
        compiler_params=pltpu.CompilerParams(vmem_limit_bytes=4 * 2**20),
    )(*pieces, *states)


def finish_kernel(parts, logits, out, normalizer, done, sems):
    top = jnp.max(parts[...], axis=0, keepdims=True)
    whole = top + jnp.log(jnp.sum(jnp.exp(parts[...] - top), axis=0, keepdims=True))
    normalizer[...] = whole
    columns = logits.shape[0]
    tile = row_tile(columns)
    copies = []
    for t in range(columns // tile):
        span = pl.ds(t * tile, tile)
        part = logits[span, :]
        done[span, :] = jnp.where(part > reachable, part - whole, 0.0)
        copies.append(pltpu.make_async_copy(done.at[span, :], out.at[span, :], sems.at[t]))
        copies[-1].start()
    for copy in copies:
        copy.wait()


def finish(parts, logits):
    columns, all_rows = logits.shape
    vmem = pl.BlockSpec(memory_space=pltpu.VMEM)
    return pl.pallas_call(
        finish_kernel,
        in_specs=[vmem] * 2,
        out_specs=[pl.BlockSpec(memory_space=pltpu.HBM), vmem],
        out_shape=[
            jax.ShapeDtypeStruct((columns, all_rows), jnp.float32),
            jax.ShapeDtypeStruct((1, all_rows), jnp.float32),
        ],
        scratch_shapes=[
            pltpu.VMEM((columns, all_rows), jnp.float32),
            pltpu.SemaphoreType.DMA((columns // row_tile(columns),)),
        ],
        compiler_params=pltpu.CompilerParams(vmem_limit_bytes=7 * 2**20),
    )(parts, pltpu.with_memory_space_constraint(logits, pltpu.VMEM))


def local(rows_count, vocab_count, hidden_rows, row_states, head_weight, grammar_table):
    block, depth = hidden_rows.shape
    columns = head_weight.shape[1]
    half = vocab_count // 2
    all_rows = block * vocab_count
    weight, table = head_weight.T, grammar_table.T

    row_states = row_states.reshape(1, block)
    pieces = [hidden_rows] + [swap(hidden_rows, "vocab", vocab_count, d) for d in range(1, vocab_count)]
    states = [row_states] + [swap(row_states, "vocab", vocab_count, 2 * d) for d in range(1, half)]
    plan = dict(
        vocab_count=vocab_count,
        sizes=(rows_count, block, depth, columns, all_rows),
        load=[(0, 0)],
        compute=[],
        load_table=True,
        first=False,
        mask=False,
        last=False,
    )
    held, rules = stage(plan, weight, table, None, None, None, None, [])
    pieces, states, held, rules = lax.optimization_barrier((pieces, states, held, rules))
    own, near = join(pieces, states)
    states = [near, swap(near, "vocab", vocab_count, 1)]

    order = ring_order(rows_count)
    ahead = [(order[i], order[(i + 1) % rows_count]) for i in range(rows_count)]
    back = [(b, a) for a, b in ahead]
    last_hop = rows_count // 2
    acc, load, used = None, plan["load"], 1
    arrived = [(0, own)]
    up = down = own
    for j in range(1, last_hop + 2):
        coming = []
        if j < last_hop:
            coming = [(-j, lax.ppermute(up, "rows", ahead)), (j, lax.ppermute(down, "rows", back))]
        elif j == last_hop:
            coming = [(j, lax.ppermute(up, "rows", ahead))]
        compute = [slot for _, slot in load]
        rows = [piece for _, piece in arrived]
        load = [(offset, (used + i) % slots) for i, (offset, _) in enumerate(coming)]
        used += len(load)
        plan = dict(
            vocab_count=vocab_count,
            sizes=(rows_count, block, depth, columns, all_rows),
            load=load,
            compute=compute,
            load_table=False,
            first=j == 1,
            mask=j == 2,
            last=j > last_hop,
        )
        res = list(stage(plan, weight, table, rules, states, held, acc, rows))
        held, acc = res[:2]
        if plan["last"]:
            lse = res[2]
        else:
            pieces, states, held, acc = lax.optimization_barrier(([p for _, p in coming], states, held, acc))
            arrived = [(offset, p) for (offset, _), p in zip(coming, pieces)]
            up, down = pieces[0], pieces[-1]

    count = rows_count * vocab_count
    sent = jnp.broadcast_to(lse[None], (count, 1, all_rows))
    parts = lax.all_to_all(sent, ("rows", "vocab"), 0, 0, tiled=True)
    log_probs, normalizer = finish(parts.reshape(count, all_rows), acc)
    return log_probs.T, normalizer.reshape(all_rows)


def solution(mesh):
    placed = (
        P("vocab", "rows"),
        P("vocab"),
        P(None, ("rows", "vocab")),
        P(None, ("rows", "vocab")),
    )
    return jax.shard_map(
        functools.partial(local, mesh.shape["rows"], mesh.shape["vocab"]),
        mesh=mesh,
        in_specs=placed,
        out_specs=(P(None, ("rows", "vocab")), P()),
        check_vma=False,
    )
```

```python
import functools

import jax
import jax.numpy as jnp
from jax import lax
from jax.experimental import pallas as pl
from jax.experimental.pallas import tpu as pltpu
from jax.sharding import PartitionSpec as P

lowest = -1e30
reachable = -1e29
slots = 4
raw_slots = 5


def ring_order(size):
    return list(range(0, size, 2)) + list(range(1, size, 2))[::-1]


def swap(x, axis, size, distance):
    return lax.ppermute(x, axis, [(i, i ^ distance) for i in range(size)])


def row_tile(columns):
    fits = [t for t in range(16, 529, 16) if columns % t == 0]
    return max(fits) if fits else columns


def ring_place(offset, count):
    here = lax.axis_index("rows")
    half = here // 2
    spot = jnp.where(here % 2 == 0, half, count - 1 - half)
    spot = lax.rem(spot + offset + count, count)
    return jnp.where(spot < count // 2, 2 * spot, 2 * (count - 1 - spot) + 1)


def stage_kernel(plan, *refs):
    rows_count, block, depth, columns, all_rows = plan["sizes"]
    half = plan["vocab_count"] // 2
    refs = list(refs)
    take = lambda n: [refs.pop(0) for _ in range(n)]
    (weight,) = take(1)
    if plan["load_table"]:
        (table_in,) = take(1)
    else:
        take(1)
    if plan["mask"]:
        rules_in, near, far = take(3)
    if plan["compute"] and not plan["first"]:
        take(1)
    chunks = [(slot, take(1)[0]) for slot in plan["compute"]]
    (held,) = take(1)
    acc = take(1)[0] if plan["compute"] else None
    lse = take(1)[0] if plan["last"] else None
    if plan["compute"]:
        turned, marks, sems = take(3)
    else:
        rules_out, raw, raw_sems, sems = take(4)

    tile = row_tile(columns)
    tiles = columns // tile
    copies = []
    for offset, slot in plan["load"]:
        way = jnp.where(lax.axis_index("vocab") % 2 == 0, offset, -offset)
        at = pl.multiple_of(ring_place(way, rows_count) * depth, depth)
        for t in range(tiles):
            span = pl.ds(t * tile, tile)
            copies.append((weight.at[span, pl.ds(at, depth)], held.at[slot, span, :]))
    copies = [pltpu.make_async_copy(a, b, sems.at[n]) for n, (a, b) in enumerate(copies)]
    if plan["compute"]:
        for copy in copies:
            copy.start()
    else:
        raw_copies = []
        for t in range(tiles):
            span = pl.ds(t * tile, tile)
            raw_copies.append(pltpu.make_async_copy(table_in.at[span, :], raw.at[t % raw_slots], raw_sems.at[t]))
        for copy in raw_copies[:raw_slots]:
            copy.start()
        for t in range(tiles):
            raw_copies[t].wait()
            copies[t].start()
            rules_out[pl.ds(t * tile, tile), :] = raw[t % raw_slots].astype(jnp.float32).astype(jnp.bfloat16)
            if t + raw_slots < tiles:
                raw_copies[t + raw_slots].start()

    if plan["compute"]:
        for c, (_, ref) in enumerate(chunks):
            turned[c] = ref[...].astype(jnp.float32).T.astype(jnp.bfloat16)
        if plan["mask"]:
            state_count = rules_in.shape[1]
            owner = lax.broadcasted_iota(jnp.int32, (1, all_rows), 1) // block
            wanted = jnp.zeros((1, all_rows), jnp.int32)
            vocab_at = lax.axis_index("vocab")
            for other, ref in enumerate((near, far)):
                for j in range(half):
                    part = jnp.tile(ref[:, j * block : (j + 1) * block], (1, all_rows // block))
                    wanted = jnp.where(owner == (vocab_at ^ (2 * j + other)), part, wanted)
            state = lax.broadcasted_iota(jnp.int32, (state_count, all_rows), 0)
            marks[...] = (state == wanted).astype(jnp.float32).astype(jnp.bfloat16)

        def work(t, carry):
            span = pl.ds(pl.multiple_of(t * tile, tile), tile) if tiles > 1 else slice(None)
            total = 0.0 if plan["first"] else acc[span, :]
            if plan["mask"]:
                allowed = jnp.dot(rules_in[span, :], marks[...], preferred_element_type=jnp.float32) > 0.5
                total = jnp.where(allowed, total, lowest)
            for c, (slot, _) in enumerate(chunks):
                total += jnp.dot(held[slot, span, :], turned[c], preferred_element_type=jnp.float32)
            acc[span, :] = total
            if plan["last"]:
                peak, exps = carry
                new_peak = jnp.maximum(peak, jnp.max(total, axis=0, keepdims=True))
                terms = jnp.where(total > reachable, jnp.exp(total - new_peak), 0.0)
                exps = exps * jnp.exp(peak - new_peak) + jnp.sum(terms, axis=0, keepdims=True)
                return new_peak, exps
            return carry

        start = ()
        if plan["last"]:
            start = (jnp.full((1, all_rows), lowest, jnp.float32), jnp.zeros((1, all_rows), jnp.float32))
        done = lax.fori_loop(0, tiles, work, start, unroll=True)
        if plan["last"]:
            peak, exps = done
            lse[...] = jnp.where(exps > 0.0, peak + jnp.log(exps), lowest)

    for copy in copies:
        copy.wait()


def stage(plan, weight, table, rules, states, held, acc, rows):
    rows_count, block, depth, columns, all_rows = plan["sizes"]
    vmem = pl.BlockSpec(memory_space=pltpu.VMEM)
    keep = lambda x: pltpu.with_memory_space_constraint(x, pltpu.VMEM)
    args, specs, out, alias = [weight], [pl.BlockSpec(memory_space=pl.ANY)], [], {}
    state_count = table.shape[1]
    if plan["load_table"]:
        args.append(pltpu.with_memory_space_constraint(table, pltpu.HBM))
        specs.append(pl.BlockSpec(memory_space=pltpu.HBM))
    else:
        alias[len(args)] = 0
        args.append(keep(held))
        specs.append(vmem)
    if plan["mask"]:
        args += [keep(rules), *states]
        specs += [vmem] * 3
    if plan["compute"] and not plan["first"]:
        alias[len(args)] = 1
        args.append(keep(acc))
        specs.append(vmem)
    args += rows
    specs += [vmem] * len(rows)
    out.append(pltpu.VMEM((slots, columns, depth), jnp.bfloat16))
    if plan["compute"]:
        out.append(pltpu.VMEM((columns, all_rows), jnp.float32))
    if plan["last"]:
        out.append(jax.ShapeDtypeStruct((1, all_rows), jnp.float32))
    tile = row_tile(columns)
    tiles = columns // tile
    sems = pltpu.SemaphoreType.DMA((max(1, tiles * len(plan["load"])),))
    if plan["compute"]:
        scratch = [
            pltpu.VMEM((len(plan["compute"]), depth, all_rows), jnp.bfloat16),
            pltpu.VMEM((state_count, all_rows), jnp.bfloat16),
            sems,
        ]
    else:
        out.append(pltpu.VMEM((columns, state_count), jnp.bfloat16))
        scratch = [
            pltpu.VMEM((raw_slots, tile, state_count), jnp.int32),
            pltpu.SemaphoreType.DMA((tiles,)),
            sems,
        ]
    moved = 2 * columns * depth * len(plan["load"]) + 4 * columns * state_count * plan["load_table"]
    return pl.pallas_call(
        functools.partial(stage_kernel, plan),
        in_specs=specs,
        out_shape=out,
        out_specs=[vmem] * len(out),
        input_output_aliases=alias,
        scratch_shapes=scratch,
        compiler_params=pltpu.CompilerParams(vmem_limit_bytes=7 * 2**20),
        cost_estimate=pl.CostEstimate(
            flops=2 * all_rows * depth * columns * len(plan["compute"]),
            bytes_accessed=moved,
            transcendentals=all_rows * columns * plan["last"],
        ),
    )(*args)


def join_kernel(vocab_count, *refs):
    pieces, states = refs[:vocab_count], refs[vocab_count:-2]
    rows, near = refs[-2:]
    block = pieces[0].shape[0]
    vocab_at = lax.axis_index("vocab")
    for d, ref in enumerate(pieces):
        rows[pl.ds(pl.multiple_of((vocab_at ^ d) * block, block), block), :] = ref[...]
    width = near.shape[1]
    owner = lax.broadcasted_iota(jnp.int32, (1, width), 1) // block
    joined = jnp.zeros((1, width), jnp.int32)
    for j, ref in enumerate(states):
        joined = jnp.where(owner == j, jnp.tile(ref[...], (1, width // block)), joined)
    near[...] = joined


def join(pieces, states):
    block, depth = pieces[0].shape
    width = -(-block * len(states) // 128) * 128
    vmem = pl.BlockSpec(memory_space=pltpu.VMEM)
    return pl.pallas_call(
        functools.partial(join_kernel, len(pieces)),
        in_specs=[vmem] * (len(pieces) + len(states)),
        out_specs=[vmem] * 2,
        out_shape=[
            jax.ShapeDtypeStruct((block * len(pieces), depth), jnp.bfloat16),
            jax.ShapeDtypeStruct((1, width), jnp.int32),
        ],
        compiler_params=pltpu.CompilerParams(vmem_limit_bytes=4 * 2**20),
    )(*pieces, *states)


def local(rows_count, vocab_count, hidden_rows, row_states, head_weight, grammar_table):
    block, depth = hidden_rows.shape
    columns = head_weight.shape[1]
    half = vocab_count // 2
    all_rows = block * vocab_count
    weight, table = head_weight.T, grammar_table.T

    row_states = row_states.reshape(1, block)
    pieces = [hidden_rows] + [swap(hidden_rows, "vocab", vocab_count, d) for d in range(1, vocab_count)]
    states = [row_states] + [swap(row_states, "vocab", vocab_count, 2 * d) for d in range(1, half)]
    plan = dict(
        vocab_count=vocab_count,
        sizes=(rows_count, block, depth, columns, all_rows),
        load=[(0, 0)],
        compute=[],
        load_table=True,
        first=False,
        mask=False,
        last=False,
    )
    held, rules = stage(plan, weight, table, None, None, None, None, [])
    pieces, states, held, rules = lax.optimization_barrier((pieces, states, held, rules))
    own, near = join(pieces, states)
    states = [near, swap(near, "vocab", vocab_count, 1)]

    order = ring_order(rows_count)
    onward = [
        (order[i] * vocab_count + v, order[(i + (-1 if v % 2 else 1)) % rows_count] * vocab_count + v)
        for i in range(rows_count)
        for v in range(vocab_count)
    ]
    last_hop = rows_count // 2
    acc, load, used = None, plan["load"], 1
    rows, piece = [own], own
    for j in range(1, last_hop + 2):
        offsets = []
        if j <= last_hop:
            piece = lax.ppermute(piece, ("rows", "vocab"), onward)
            offsets = [-j, j] if j < last_hop else [j]
        compute = [slot for _, slot in load]
        load = [(offset, (used + i) % slots) for i, offset in enumerate(offsets)]
        used += len(load)
        plan = dict(
            vocab_count=vocab_count,
            sizes=(rows_count, block, depth, columns, all_rows),
            load=load,
            compute=compute,
            load_table=False,
            first=j == 1,
            mask=j == 2,
            last=j > last_hop,
        )
        res = list(stage(plan, weight, table, rules, states, held, acc, rows))
        held, acc = res[:2]
        if j <= last_hop:
            piece, states, held, acc = lax.optimization_barrier((piece, states, held, acc))
            rows = [piece] + ([swap(piece, "vocab", vocab_count, 1)] if j < last_hop else [])

    lse = res[2]
    count = rows_count * vocab_count
    sent = jnp.broadcast_to(lse[None], (count, 1, all_rows))
    parts = lax.all_to_all(sent, ("rows", "vocab"), 0, 0, tiled=True)
    top = jnp.max(parts, axis=0)
    lse = top + jnp.log(jnp.sum(jnp.exp(parts - top), axis=0))
    log_probs = jnp.where(acc > reachable, acc - lse, 0.0)
    return log_probs.T, lse.reshape(all_rows)


def solution(mesh):
    placed = (
        P("vocab", "rows"),
        P("vocab"),
        P(None, ("rows", "vocab")),
        P(None, ("rows", "vocab")),
    )
    return jax.shard_map(
        functools.partial(local, mesh.shape["rows"], mesh.shape["vocab"]),
        mesh=mesh,
        in_specs=placed,
        out_specs=(P(None, ("rows", "vocab")), P()),
        check_vma=False,
    )
```

```python
import functools

import jax
import jax.numpy as jnp
from jax import lax
from jax.experimental import pallas as pl
from jax.experimental.pallas import tpu as pltpu
from jax.sharding import PartitionSpec as P

lowest = -1e30
reachable = -1e29
slots = 4
raw_slots = 5


def ring_order(size):
    return list(range(0, size, 2)) + list(range(1, size, 2))[::-1]


def swap(x, axis, size, distance):
    return lax.ppermute(x, axis, [(i, i ^ distance) for i in range(size)])


def row_tile(columns):
    fits = [t for t in range(16, 529, 16) if columns % t == 0]
    return max(fits) if fits else columns


def ring_place(offset, count):
    here = lax.axis_index("rows")
    half = here // 2
    spot = jnp.where(here % 2 == 0, half, count - 1 - half)
    spot = lax.rem(spot + offset + count, count)
    return jnp.where(spot < count // 2, 2 * spot, 2 * (count - 1 - spot) + 1)


def stage_kernel(plan, *refs):
    rows_count, block, depth, columns, all_rows = plan["sizes"]
    half = plan["vocab_count"] // 2
    refs = list(refs)
    take = lambda n: [refs.pop(0) for _ in range(n)]
    (weight,) = take(1)
    if plan["load_table"]:
        (table_in,) = take(1)
    else:
        take(1)
    if plan["mask"]:
        rules_in, near, far = take(3)
    if plan["compute"] and not plan["first"]:
        take(1)
    chunks = [(slot, take(1)[0]) for slot in plan["compute"]]
    (held,) = take(1)
    acc = take(1)[0] if plan["compute"] else None
    lse = take(1)[0] if plan["last"] else None
    if plan["compute"]:
        turned, marks, sems = take(3)
    else:
        rules_out, raw, raw_sems, sems = take(4)

    tile = row_tile(columns)
    tiles = columns // tile
    copies = []
    for offset, slot, first, last in plan["late"] + plan["load"]:
        way = jnp.where(lax.axis_index("vocab") % 2 == 0, offset, -offset)
        at = pl.multiple_of(ring_place(way, rows_count) * depth, depth)
        for t in range(first, last):
            span = pl.ds(t * tile, tile)
            copies.append((weight.at[span, pl.ds(at, depth)], held.at[slot, span, :]))
    copies = [pltpu.make_async_copy(a, b, sems.at[n]) for n, (a, b) in enumerate(copies)]
    late = sum(last - first for _, _, first, last in plan["late"])
    if plan["compute"]:
        for copy in copies[:late] if late else copies:
            copy.start()
    else:
        raw_copies = []
        for t in range(tiles):
            span = pl.ds(t * tile, tile)
            raw_copies.append(pltpu.make_async_copy(table_in.at[span, :], raw.at[t % raw_slots], raw_sems.at[t]))
        for copy in raw_copies[:raw_slots]:
            copy.start()
        for t in range(tiles):
            raw_copies[t].wait()
            copies[t].start()
            rules_out[pl.ds(t * tile, tile), :] = raw[t % raw_slots].astype(jnp.float32).astype(jnp.bfloat16)
            if t + raw_slots < tiles:
                raw_copies[t + raw_slots].start()

    if plan["compute"]:
        for c, (_, ref) in enumerate(chunks):
            turned[c] = ref[...].astype(jnp.float32).T.astype(jnp.bfloat16)
        if plan["mask"]:
            state_count = rules_in.shape[1]
            owner = lax.broadcasted_iota(jnp.int32, (1, all_rows), 1) // block
            wanted = jnp.zeros((1, all_rows), jnp.int32)
            vocab_at = lax.axis_index("vocab")
            for other, ref in enumerate((near, far)):
                for j in range(half):
                    part = jnp.tile(ref[:, j * block : (j + 1) * block], (1, all_rows // block))
                    wanted = jnp.where(owner == (vocab_at ^ (2 * j + other)), part, wanted)
            state = lax.broadcasted_iota(jnp.int32, (state_count, all_rows), 0)
            marks[...] = (state == wanted).astype(jnp.float32).astype(jnp.bfloat16)

        def work(t, carry):
            span = pl.ds(pl.multiple_of(t * tile, tile), tile) if tiles > 1 else slice(None)
            total = 0.0 if plan["first"] else acc[span, :]
            if plan["mask"]:
                allowed = jnp.dot(rules_in[span, :], marks[...], preferred_element_type=jnp.float32) > 0.5
                total = jnp.where(allowed, total, lowest)
            for c, (slot, _) in enumerate(chunks):
                total += jnp.dot(held[slot, span, :], turned[c], preferred_element_type=jnp.float32)
            acc[span, :] = total
            if plan["last"]:
                peak, exps = carry
                new_peak = jnp.maximum(peak, jnp.max(total, axis=0, keepdims=True))
                terms = jnp.where(total > reachable, jnp.exp(total - new_peak), 0.0)
                exps = exps * jnp.exp(peak - new_peak) + jnp.sum(terms, axis=0, keepdims=True)
                return new_peak, exps
            return carry

        start = ()
        if plan["last"]:
            start = (jnp.full((1, all_rows), lowest, jnp.float32), jnp.zeros((1, all_rows), jnp.float32))
        if late:
            done = lax.fori_loop(0, (tiles - late) // 2, work, start, unroll=True)
            for copy in copies[late:]:
                copy.start()
            done = lax.fori_loop((tiles - late) // 2, tiles - late, work, done, unroll=True)
            for copy in copies[:late]:
                copy.wait()
            copies = copies[late:]
            done = lax.fori_loop(tiles - late, tiles, work, done, unroll=True)
        else:
            done = lax.fori_loop(0, tiles, work, start, unroll=True)
        if plan["last"]:
            peak, exps = done
            lse[...] = jnp.where(exps > 0.0, peak + jnp.log(exps), lowest)

    for copy in copies:
        copy.wait()


def stage(plan, weight, table, rules, states, held, acc, rows):
    rows_count, block, depth, columns, all_rows = plan["sizes"]
    vmem = pl.BlockSpec(memory_space=pltpu.VMEM)
    keep = lambda x: pltpu.with_memory_space_constraint(x, pltpu.VMEM)
    args, specs, out, alias = [weight], [pl.BlockSpec(memory_space=pl.ANY)], [], {}
    state_count = table.shape[1]
    if plan["load_table"]:
        args.append(pltpu.with_memory_space_constraint(table, pltpu.HBM))
        specs.append(pl.BlockSpec(memory_space=pltpu.HBM))
    else:
        alias[len(args)] = 0
        args.append(keep(held))
        specs.append(vmem)
    if plan["mask"]:
        args += [keep(rules), *states]
        specs += [vmem] * 3
    if plan["compute"] and not plan["first"]:
        alias[len(args)] = 1
        args.append(keep(acc))
        specs.append(vmem)
    args += rows
    specs += [vmem] * len(rows)
    out.append(pltpu.VMEM((slots, columns, depth), jnp.bfloat16))
    if plan["compute"]:
        out.append(pltpu.VMEM((columns, all_rows), jnp.float32))
    if plan["last"]:
        out.append(jax.ShapeDtypeStruct((1, all_rows), jnp.float32))
    tile = row_tile(columns)
    tiles = columns // tile
    sems = pltpu.SemaphoreType.DMA((max(1, tiles * len(plan["late"] + plan["load"])),))
    if plan["compute"]:
        scratch = [
            pltpu.VMEM((len(plan["compute"]), depth, all_rows), jnp.bfloat16),
            pltpu.VMEM((state_count, all_rows), jnp.bfloat16),
            sems,
        ]
    else:
        out.append(pltpu.VMEM((columns, state_count), jnp.bfloat16))
        scratch = [
            pltpu.VMEM((raw_slots, tile, state_count), jnp.int32),
            pltpu.SemaphoreType.DMA((tiles,)),
            sems,
        ]
    moved = 2 * columns * depth * len(plan["load"]) + 4 * columns * state_count * plan["load_table"]
    return pl.pallas_call(
        functools.partial(stage_kernel, plan),
        in_specs=specs,
        out_shape=out,
        out_specs=[vmem] * len(out),
        input_output_aliases=alias,
        scratch_shapes=scratch,
        compiler_params=pltpu.CompilerParams(vmem_limit_bytes=7 * 2**20),
        cost_estimate=pl.CostEstimate(
            flops=2 * all_rows * depth * columns * len(plan["compute"]),
            bytes_accessed=moved,
            transcendentals=all_rows * columns * plan["last"],
        ),
    )(*args)


def join_kernel(vocab_count, *refs):
    pieces, states = refs[:vocab_count], refs[vocab_count:-2]
    rows, near = refs[-2:]
    block = pieces[0].shape[0]
    vocab_at = lax.axis_index("vocab")
    for d, ref in enumerate(pieces):
        rows[pl.ds(pl.multiple_of((vocab_at ^ d) * block, block), block), :] = ref[...]
    width = near.shape[1]
    owner = lax.broadcasted_iota(jnp.int32, (1, width), 1) // block
    joined = jnp.zeros((1, width), jnp.int32)
    for j, ref in enumerate(states):
        joined = jnp.where(owner == j, jnp.tile(ref[...], (1, width // block)), joined)
    near[...] = joined


def join(pieces, states):
    block, depth = pieces[0].shape
    width = -(-block * len(states) // 128) * 128
    vmem = pl.BlockSpec(memory_space=pltpu.VMEM)
    return pl.pallas_call(
        functools.partial(join_kernel, len(pieces)),
        in_specs=[vmem] * (len(pieces) + len(states)),
        out_specs=[vmem] * 2,
        out_shape=[
            jax.ShapeDtypeStruct((block * len(pieces), depth), jnp.bfloat16),
            jax.ShapeDtypeStruct((1, width), jnp.int32),
        ],
        compiler_params=pltpu.CompilerParams(vmem_limit_bytes=4 * 2**20),
    )(*pieces, *states)


def local(rows_count, vocab_count, hidden_rows, row_states, head_weight, grammar_table):
    block, depth = hidden_rows.shape
    columns = head_weight.shape[1]
    half = vocab_count // 2
    all_rows = block * vocab_count
    weight, table = head_weight.T, grammar_table.T

    row_states = row_states.reshape(1, block)
    pieces = [hidden_rows] + [swap(hidden_rows, "vocab", vocab_count, d) for d in range(1, vocab_count)]
    states = [row_states] + [swap(row_states, "vocab", vocab_count, 2 * d) for d in range(1, half)]
    tiles = columns // row_tile(columns)
    tail = 5 * tiles // 9
    plan = dict(
        vocab_count=vocab_count,
        sizes=(rows_count, block, depth, columns, all_rows),
        load=[(0, 0, 0, tiles)],
        late=[],
        compute=[],
        load_table=True,
        first=False,
        mask=False,
        last=False,
    )
    held, rules = stage(plan, weight, table, None, None, None, None, [])
    pieces, states, held, rules = lax.optimization_barrier((pieces, states, held, rules))
    own, near = join(pieces, states)
    states = [near, swap(near, "vocab", vocab_count, 1)]

    order = ring_order(rows_count)
    onward = [
        (order[i] * vocab_count + v, order[(i + (-1 if v % 2 else 1)) % rows_count] * vocab_count + v)
        for i in range(rows_count)
        for v in range(vocab_count)
    ]
    last_hop = rows_count // 2
    acc, load, used = None, plan["load"], 1
    rows, piece = [own], own
    for j in range(1, last_hop + 2):
        offsets = []
        if j <= last_hop:
            piece = lax.ppermute(piece, ("rows", "vocab"), onward)
            offsets = [-j, j] if j < last_hop else [j]
        compute = [item[1] for item in load]
        late = [(load[1][0], load[1][1], tiles - tail, tiles)] if tail and j == last_hop else []
        load = [(offset, (used + i) % slots, 0, tiles) for i, offset in enumerate(offsets)]
        used += len(load)
        if tail and j == last_hop - 1:
            load[1] = load[1][:3] + (tiles - tail,)
        plan = dict(
            vocab_count=vocab_count,
            sizes=(rows_count, block, depth, columns, all_rows),
            load=load,
            late=late,
            compute=compute,
            load_table=False,
            first=j == 1,
            mask=j == 2,
            last=j > last_hop,
        )
        res = list(stage(plan, weight, table, rules, states, held, acc, rows))
        held, acc = res[:2]
        if j <= last_hop:
            piece, states, held, acc = lax.optimization_barrier((piece, states, held, acc))
            rows = [piece] + ([swap(piece, "vocab", vocab_count, 1)] if j < last_hop else [])

    lse = res[2]
    count = rows_count * vocab_count
    sent = jnp.broadcast_to(lse[None], (count, 1, all_rows))
    parts = lax.all_to_all(sent, ("rows", "vocab"), 0, 0, tiled=True)
    top = jnp.max(parts, axis=0)
    lse = top + jnp.log(jnp.sum(jnp.exp(parts - top), axis=0))
    log_probs = jnp.where(acc > reachable, acc - lse, 0.0)
    return log_probs.T, lse.reshape(all_rows)


def solution(mesh):
    placed = (
        P("vocab", "rows"),
        P("vocab"),
        P(None, ("rows", "vocab")),
        P(None, ("rows", "vocab")),
    )
    return jax.shard_map(
        functools.partial(local, mesh.shape["rows"], mesh.shape["vocab"]),
        mesh=mesh,
        in_specs=placed,
        out_specs=(P(None, ("rows", "vocab")), P()),
        check_vma=False,
    )
```

```python
import functools

import jax
import jax.numpy as jnp
from jax import lax
from jax.experimental import pallas as pl
from jax.experimental.pallas import tpu as pltpu
from jax.sharding import PartitionSpec as P

lowest = -1e30
reachable = -1e29
slots = 4
raw_slots = 5


def ring_order(size):
    return list(range(0, size, 2)) + list(range(1, size, 2))[::-1]


def swap(x, axis, size, distance):
    return lax.ppermute(x, axis, [(i, i ^ distance) for i in range(size)])


def row_tile(columns):
    fits = [t for t in range(16, 529, 16) if columns % t == 0]
    return max(fits) if fits else columns


def ring_place(offset, count):
    here = lax.axis_index("rows")
    half = here // 2
    spot = jnp.where(here % 2 == 0, half, count - 1 - half)
    spot = lax.rem(spot + offset + count, count)
    return jnp.where(spot < count // 2, 2 * spot, 2 * (count - 1 - spot) + 1)


def stage_kernel(plan, *refs):
    rows_count, block, depth, columns, all_rows = plan["sizes"]
    half = plan["vocab_count"] // 2
    refs = list(refs)
    take = lambda n: [refs.pop(0) for _ in range(n)]
    (weight,) = take(1)
    if plan["load_table"]:
        (table_in,) = take(1)
    else:
        take(1)
    if plan["mask"]:
        rules_in, near, far = take(3)
    if plan["compute"] and not plan["first"]:
        take(1)
    chunks = [(slot, take(1)[0]) for slot in plan["compute"]]
    (held,) = take(1)
    acc = take(1)[0] if plan["compute"] else None
    lse = take(1)[0] if plan["last"] else None
    if plan["compute"]:
        turned, marks, sems = take(3)
    else:
        rules_out, raw, raw_sems, sems = take(4)

    tile = row_tile(columns)
    tiles = columns // tile
    copies = []
    for offset, slot, first, last in plan["late"] + plan["load"]:
        way = jnp.where(lax.axis_index("vocab") % 2 == 0, offset, -offset)
        at = pl.multiple_of(ring_place(way, rows_count) * depth, depth)
        for t in range(first, last):
            span = pl.ds(t * tile, tile)
            copies.append((weight.at[span, pl.ds(at, depth)], held.at[slot, span, :]))
    copies = [pltpu.make_async_copy(a, b, sems.at[n]) for n, (a, b) in enumerate(copies)]
    late = sum(last - first for _, _, first, last in plan["late"])
    if plan["compute"]:
        for copy in copies[:late] if late else copies:
            copy.start()
    else:
        raw_copies = []
        for t in range(tiles):
            span = pl.ds(t * tile, tile)
            raw_copies.append(pltpu.make_async_copy(table_in.at[span, :], raw.at[t % raw_slots], raw_sems.at[t]))
        for copy in raw_copies[:raw_slots]:
            copy.start()
        for t in range(tiles):
            raw_copies[t].wait()
            copies[t].start()
            rules_out[pl.ds(t * tile, tile), :] = raw[t % raw_slots].astype(jnp.float32).astype(jnp.bfloat16)
            if t + raw_slots < tiles:
                raw_copies[t + raw_slots].start()

    if plan["compute"]:
        for c, (_, ref) in enumerate(chunks):
            turned[c] = ref[...].astype(jnp.float32).T.astype(jnp.bfloat16)
        if plan["mask"]:
            state_count = rules_in.shape[1]
            owner = lax.broadcasted_iota(jnp.int32, (1, all_rows), 1) // block
            wanted = jnp.zeros((1, all_rows), jnp.int32)
            vocab_at = lax.axis_index("vocab")
            for other, ref in enumerate((near, far)):
                for j in range(half):
                    part = jnp.tile(ref[:, j * block : (j + 1) * block], (1, all_rows // block))
                    wanted = jnp.where(owner == (vocab_at ^ (2 * j + other)), part, wanted)
            state = lax.broadcasted_iota(jnp.int32, (state_count, all_rows), 0)
            marks[...] = (state == wanted).astype(jnp.float32).astype(jnp.bfloat16)

        def work(t, carry):
            span = pl.ds(pl.multiple_of(t * tile, tile), tile) if tiles > 1 else slice(None)
            total = 0.0 if plan["first"] else acc[span, :]
            if plan["mask"]:
                allowed = jnp.dot(rules_in[span, :], marks[...], preferred_element_type=jnp.float32) > 0.5
                total = jnp.where(allowed, total, lowest)
            for c, (slot, _) in enumerate(chunks):
                total += jnp.dot(held[slot, span, :], turned[c], preferred_element_type=jnp.float32)
            acc[span, :] = total
            if plan["last"]:
                peak, exps = carry
                new_peak = jnp.maximum(peak, jnp.max(total, axis=0, keepdims=True))
                terms = jnp.where(total > reachable, jnp.exp(total - new_peak), 0.0)
                exps = exps * jnp.exp(peak - new_peak) + jnp.sum(terms, axis=0, keepdims=True)
                return new_peak, exps
            return carry

        start = ()
        if plan["last"]:
            start = (jnp.full((1, all_rows), lowest, jnp.float32), jnp.zeros((1, all_rows), jnp.float32))
        if late:
            done = lax.fori_loop(0, tiles // 3, work, start, unroll=True)
            for copy in copies[:late]:
                copy.wait()
            copies = copies[late:]
            for copy in copies:
                copy.start()
            done = lax.fori_loop(tiles // 3, tiles, work, done, unroll=True)
        else:
            done = lax.fori_loop(0, tiles, work, start, unroll=True)
        if plan["last"]:
            peak, exps = done
            lse[...] = jnp.where(exps > 0.0, peak + jnp.log(exps), lowest)

    for copy in copies:
        copy.wait()


def stage(plan, weight, table, rules, states, held, acc, rows):
    rows_count, block, depth, columns, all_rows = plan["sizes"]
    vmem = pl.BlockSpec(memory_space=pltpu.VMEM)
    keep = lambda x: pltpu.with_memory_space_constraint(x, pltpu.VMEM)
    args, specs, out, alias = [weight], [pl.BlockSpec(memory_space=pl.ANY)], [], {}
    state_count = table.shape[1]
    if plan["load_table"]:
        args.append(pltpu.with_memory_space_constraint(table, pltpu.HBM))
        specs.append(pl.BlockSpec(memory_space=pltpu.HBM))
    else:
        alias[len(args)] = 0
        args.append(keep(held))
        specs.append(vmem)
    if plan["mask"]:
        args += [keep(rules), *states]
        specs += [vmem] * 3
    if plan["compute"] and not plan["first"]:
        alias[len(args)] = 1
        args.append(keep(acc))
        specs.append(vmem)
    args += rows
    specs += [vmem] * len(rows)
    out.append(pltpu.VMEM((slots, columns, depth), jnp.bfloat16))
    if plan["compute"]:
        out.append(pltpu.VMEM((columns, all_rows), jnp.float32))
    if plan["last"]:
        out.append(jax.ShapeDtypeStruct((1, all_rows), jnp.float32))
    tile = row_tile(columns)
    tiles = columns // tile
    sems = pltpu.SemaphoreType.DMA((max(1, tiles * len(plan["late"] + plan["load"])),))
    if plan["compute"]:
        scratch = [
            pltpu.VMEM((len(plan["compute"]), depth, all_rows), jnp.bfloat16),
            pltpu.VMEM((state_count, all_rows), jnp.bfloat16),
            sems,
        ]
    else:
        out.append(pltpu.VMEM((columns, state_count), jnp.bfloat16))
        scratch = [
            pltpu.VMEM((raw_slots, tile, state_count), jnp.int32),
            pltpu.SemaphoreType.DMA((tiles,)),
            sems,
        ]
    moved = 2 * columns * depth * len(plan["load"]) + 4 * columns * state_count * plan["load_table"]
    return pl.pallas_call(
        functools.partial(stage_kernel, plan),
        in_specs=specs,
        out_shape=out,
        out_specs=[vmem] * len(out),
        input_output_aliases=alias,
        scratch_shapes=scratch,
        compiler_params=pltpu.CompilerParams(vmem_limit_bytes=7 * 2**20),
        cost_estimate=pl.CostEstimate(
            flops=2 * all_rows * depth * columns * len(plan["compute"]),
            bytes_accessed=moved,
            transcendentals=all_rows * columns * plan["last"],
        ),
    )(*args)


def join_kernel(vocab_count, *refs):
    pieces, states = refs[:vocab_count], refs[vocab_count:-2]
    rows, near = refs[-2:]
    block = pieces[0].shape[0]
    vocab_at = lax.axis_index("vocab")
    for d, ref in enumerate(pieces):
        rows[pl.ds(pl.multiple_of((vocab_at ^ d) * block, block), block), :] = ref[...]
    width = near.shape[1]
    owner = lax.broadcasted_iota(jnp.int32, (1, width), 1) // block
    joined = jnp.zeros((1, width), jnp.int32)
    for j, ref in enumerate(states):
        joined = jnp.where(owner == j, jnp.tile(ref[...], (1, width // block)), joined)
    near[...] = joined


def join(pieces, states):
    block, depth = pieces[0].shape
    width = -(-block * len(states) // 128) * 128
    vmem = pl.BlockSpec(memory_space=pltpu.VMEM)
    return pl.pallas_call(
        functools.partial(join_kernel, len(pieces)),
        in_specs=[vmem] * (len(pieces) + len(states)),
        out_specs=[vmem] * 2,
        out_shape=[
            jax.ShapeDtypeStruct((block * len(pieces), depth), jnp.bfloat16),
            jax.ShapeDtypeStruct((1, width), jnp.int32),
        ],
        compiler_params=pltpu.CompilerParams(vmem_limit_bytes=4 * 2**20),
    )(*pieces, *states)


def local(rows_count, vocab_count, hidden_rows, row_states, head_weight, grammar_table):
    block, depth = hidden_rows.shape
    columns = head_weight.shape[1]
    half = vocab_count // 2
    all_rows = block * vocab_count
    weight, table = head_weight.T, grammar_table.T

    row_states = row_states.reshape(1, block)
    pieces = [hidden_rows] + [swap(hidden_rows, "vocab", vocab_count, d) for d in range(1, vocab_count)]
    states = [row_states] + [swap(row_states, "vocab", vocab_count, 2 * d) for d in range(1, half)]
    tiles = columns // row_tile(columns)
    tail = 4 * tiles // 9
    plan = dict(
        vocab_count=vocab_count,
        sizes=(rows_count, block, depth, columns, all_rows),
        load=[(0, 0, 0, tiles)],
        late=[],
        compute=[],
        load_table=True,
        first=False,
        mask=False,
        last=False,
    )
    held, rules = stage(plan, weight, table, None, None, None, None, [])
    pieces, states, held, rules = lax.optimization_barrier((pieces, states, held, rules))
    own, near = join(pieces, states)
    states = [near, swap(near, "vocab", vocab_count, 1)]

    order = ring_order(rows_count)
    onward = [
        (order[i] * vocab_count + v, order[(i + (-1 if v % 2 else 1)) % rows_count] * vocab_count + v)
        for i in range(rows_count)
        for v in range(vocab_count)
    ]
    last_hop = rows_count // 2
    acc, load, used = None, plan["load"], 1
    rows, piece = [own], own
    for j in range(1, last_hop + 2):
        offsets = []
        if j <= last_hop:
            piece = lax.ppermute(piece, ("rows", "vocab"), onward)
            offsets = [-j, j] if j < last_hop else [j]
        compute = [item[1] for item in load]
        late = [(load[1][0], load[1][1], tiles - tail, tiles)] if tail and j == last_hop else []
        load = [(offset, (used + i) % slots, 0, tiles) for i, offset in enumerate(offsets)]
        used += len(load)
        if tail and j == last_hop - 1:
            load[1] = load[1][:3] + (tiles - tail,)
        plan = dict(
            vocab_count=vocab_count,
            sizes=(rows_count, block, depth, columns, all_rows),
            load=load,
            late=late,
            compute=compute,
            load_table=False,
            first=j == 1,
            mask=j == 2,
            last=j > last_hop,
        )
        res = list(stage(plan, weight, table, rules, states, held, acc, rows))
        held, acc = res[:2]
        if j <= last_hop:
            piece, states, held, acc = lax.optimization_barrier((piece, states, held, acc))
            rows = [piece] + ([swap(piece, "vocab", vocab_count, 1)] if j < last_hop else [])

    lse = res[2]
    count = rows_count * vocab_count
    sent = jnp.broadcast_to(lse[None], (count, 1, all_rows))
    parts = lax.all_to_all(sent, ("rows", "vocab"), 0, 0, tiled=True)
    top = jnp.max(parts, axis=0)
    lse = top + jnp.log(jnp.sum(jnp.exp(parts - top), axis=0))
    log_probs = jnp.where(acc > reachable, acc - lse, 0.0)
    return log_probs.T, lse.reshape(all_rows)


def solution(mesh):
    placed = (
        P("vocab", "rows"),
        P("vocab"),
        P(None, ("rows", "vocab")),
        P(None, ("rows", "vocab")),
    )
    return jax.shard_map(
        functools.partial(local, mesh.shape["rows"], mesh.shape["vocab"]),
        mesh=mesh,
        in_specs=placed,
        out_specs=(P(None, ("rows", "vocab")), P()),
        check_vma=False,
    )
```
